128 devices in a mesh: rank: 4 (over z), tiles: 32 (over x, y, core).
Axes of the slice: x: 4, y: 4, z: 4, core: 2. Of those that a mesh axis runs over, the one named last changes fastest.
Arguments:
- user_factor: bfloat16 [32768, 1024], P('tiles', 'rank'), may hold values from -1 to 1
- item_factor: bfloat16 [8192, 1024], P('tiles', 'rank'), may hold values from -1 to 1
- context_factor: bfloat16 [256, 1024], P(None, 'rank'), may hold values from -5 to 5
- tile_user: int32 [4096], P('tiles'), may hold values from 0 to 7
- tile_item: int32 [4096], P('tiles'), may hold values from 0 to 63
- tile_context: int32 [4096], P('tiles'), may hold values from 0 to 255
- tile_count: int32 [32], P('tiles'), may hold values from 32 to 128, as said below
- tile_mask: int32 [4096, 128, 128], P('tiles'), may hold values 0 or 1
- item_slot: int32 [64], replicated, may hold values from 0 to 63, each once
Outputs:
- user_grad: float32 [32768, 1024], P('tiles', 'rank')
- item_grad: float32 [8192, 1024], P('tiles', 'rank')
- context_grad: float32 [256, 1024], P(None, 'rank')
The draws below stay inside these ranges and needn't reach their ends.
Inputs may be any that keep to these rules, and one draw needn't show every extreme that they name: `tile_count`: some index of tiles uses all 128 slots in every draw.
All inputs are finite; a program needn't handle non-finite values. No bound on the sum of `tile_mask` on one device may be relied on, other than what follows from the above.
Results may differ from the reference program's by a relative error of at most 0.0031.
Values may be sent and summed in bfloat16 or wider, within the bound.
A program may use at most 128 MiB of HBM per device.

```python
import jax
import jax.numpy as jnp
from jax import lax

R = 1024
CTX = 256
BLK = 128
UB_DEV = 8
TCAP = 128
USERS = 32768
ITEMS = 8192
IBLOCKS = 64
TILES = 4096
N_TILES = 32


def draw_tile_count(key, part):
    key = jax.random.fold_in(key, 7)
    values = jax.random.randint(key, (N_TILES,), TCAP // 4, TCAP + 1)
    where = jax.random.randint(jax.random.fold_in(key, 1), (), 0, N_TILES)
    return values.at[where].set(TCAP).astype(jnp.int32)


def set_ends(drawn, key, low, high):
    index_at = [jax.random.randint(jax.random.fold_in(key, axis), (), 0, length) for axis, length in enumerate(drawn.shape)]
    main_axis = drawn.shape.index(max(drawn.shape))
    beside = index_at[:main_axis] + [(index_at[main_axis] + 1) % drawn.shape[main_axis]] + index_at[main_axis + 1:]
    return drawn.at[tuple(index_at)].set(low).at[tuple(beside)].set(high)


def block_scale(key, extent, shards, low, top_value):
    gain, own = 1.0, jax.random.fold_in(key, 6)
    for axis_at, blocks in shards:
        heights = jnp.exp(jax.random.uniform(jax.random.fold_in(own, axis_at), (blocks,), jnp.float32, low / len(shards), top_value / len(shards)))
        gain = gain * jnp.repeat(heights, extent[axis_at] // blocks).reshape([-1 if axis == axis_at else 1 for axis in range(len(extent))])
    return gain


def gaussian(key, shape, deviation, reach, shards=(), dtype=jnp.bfloat16):
    result = deviation * jax.random.normal(key, shape, jnp.float32)
    if shards:
        result = result * block_scale(key, shape, shards, -0.22, 0.18)
    return jnp.clip(result, -reach, reach).astype(dtype)


def setup_inputs(seed: int = 0) -> dict:
    key_list = jax.random.split(jax.random.key(seed), 10)
    user_factor = gaussian(key_list[0], (USERS, R), 0.18, 1.0, ((0, 32), (1, 4)))
    item_factor = gaussian(key_list[1], (ITEMS, R), 0.18, 1.0, ((0, 32), (1, 4)))
    context_factor = gaussian(key_list[2], (CTX, R), 1.0, 5.0, ((1, 4),))
    tile_user = set_ends(jax.random.randint(key_list[3], (TILES,), 0, UB_DEV), jax.random.fold_in(key_list[3], 1), 0, UB_DEV - 1).astype(jnp.int32)
    tile_item = set_ends(jax.random.randint(key_list[4], (TILES,), 0, IBLOCKS), jax.random.fold_in(key_list[4], 1), 0, IBLOCKS - 1).astype(jnp.int32)
    tile_context = set_ends(jax.random.randint(key_list[5], (TILES,), 0, CTX), jax.random.fold_in(key_list[5], 1), 0, CTX - 1).astype(jnp.int32)
    tile_count = draw_tile_count(jax.random.fold_in(key_list[9], 71), 0)
    tile_mask = set_ends((jax.random.randint(key_list[7], (TILES, BLK, BLK), 0, 6) < 1).astype(jnp.int32), jax.random.fold_in(key_list[7], 1), 0, 1)
    item_slot = jax.random.permutation(key_list[8], IBLOCKS).astype(jnp.int32)
    return dict(user_factor=user_factor, item_factor=item_factor, context_factor=context_factor, tile_user=tile_user, tile_item=tile_item, tile_context=tile_context, tile_count=tile_count, tile_mask=tile_mask, item_slot=item_slot)


def reference(user_factor, item_factor, context_factor, tile_user, tile_item, tile_context, tile_count, tile_mask, item_slot):
    ublocks = user_factor.reshape(N_TILES, UB_DEV, BLK, R)
    iblocks = item_factor.reshape(IBLOCKS, BLK, R)
    tu = tile_user.reshape(N_TILES, TCAP)
    ti = tile_item.reshape(N_TILES, TCAP)
    tc = tile_context.reshape(N_TILES, TCAP)
    masks = tile_mask.reshape(N_TILES, TCAP, BLK, BLK)

    def one_device(carry, inputs):
        item_acc, ctx_acc = carry
        ub, tu_d, ti_d, tc_d, count, mask_d = inputs
        users = ub[tu_d]
        slots = item_slot[ti_d].astype(jnp.int32)
        items = iblocks[slots]
        crow = context_factor[tc_d].astype(jnp.float32)
        item_context = (items.astype(jnp.float32) * crow[:, None, :]).astype(jnp.bfloat16)
        user_context = (users.astype(jnp.float32) * crow[:, None, :]).astype(jnp.bfloat16)
        prediction = jnp.einsum("tur,tir->tui", users.astype(jnp.float32), item_context.astype(jnp.float32))
        live = (jnp.arange(TCAP) < count).astype(jnp.float32)[:, None, None]
        maskf = mask_d.astype(jnp.float32)
        resid = (live * (1.0 + 4.0 * maskf) * (prediction - maskf) / 128.0).astype(jnp.bfloat16)
        residf = resid.astype(jnp.float32)
        pulled = jnp.einsum("tui,tir->tur", residf, items.astype(jnp.float32))
        uterm = pulled * crow[:, None, :]
        uhot = (tu_d[:, None] == jnp.arange(UB_DEV)[None, :]).astype(jnp.float32)
        ugrad = jnp.einsum("tb,tur->bur", uhot, uterm, precision=lax.Precision.HIGHEST)
        iterm = jnp.einsum("tui,tur->tir", residf, user_context.astype(jnp.float32))
        ihot = (slots[:, None] == jnp.arange(IBLOCKS)[None, :]).astype(jnp.float32)
        item_acc = item_acc + jnp.einsum("tb,tir->bir", ihot, iterm, precision=lax.Precision.HIGHEST)
        cterm = jnp.sum(users.astype(jnp.float32) * pulled, axis=1)
        chot = (tc_d[:, None] == jnp.arange(CTX)[None, :]).astype(jnp.float32)
        ctx_acc = ctx_acc + jnp.dot(chot.T, cterm, precision=lax.Precision.HIGHEST)
        return (item_acc, ctx_acc), ugrad

    init = (jnp.zeros((IBLOCKS, BLK, R), jnp.float32), jnp.zeros((CTX, R), jnp.float32))
    (item_acc, ctx_acc), ugrads = lax.scan(one_device, init, (ublocks, tu, ti, tc, tile_count, masks))
    return ugrads.reshape(USERS, R), item_acc.reshape(ITEMS, R), ctx_acc
```

```python
import functools

import jax
import jax.numpy as jnp
from jax import lax
from jax.experimental import pallas as pl
from jax.experimental.pallas import tpu as pltpu
from jax.sharding import PartitionSpec as P

MESH = pl.DeviceIdType.MESH
BF16 = jnp.bfloat16
F32 = jnp.float32
NB = 8
PER = 4
SIDE = 128
WIDTH = 256


def kernel(
    place_ref,
    user_ref,
    perm_ref,
    live_ref,
    keep_ref,
    last_ref,
    has_ref,
    users_ref,
    shard_ref,
    crow_ref,
    mask_hbm,
    ugrad_ref,
    ipart_ref,
    cterm_ref,
    items,
    mask,
    part,
    send1,
    recv1,
    send2,
    recv2,
    resid,
    run,
    segs,
    ahot,
    icb,
    mask_sem,
    ag_send,
    ag_recv,
    z_send,
    z_recv,
):
    z = lax.axis_index("rank")
    t = lax.axis_index("tiles")
    c = lax.rem(t, 2)
    y = lax.rem(t // 2, 4)
    x = t // 8
    f = x * (1 - c) + y * c
    s = y * (1 - c) + x * c

    def dev(fi, si):
        fi, si = lax.rem(fi + 4, 4), lax.rem(si + 4, 4)
        xi = fi * (1 - c) + si * c
        yi = si * (1 - c) + fi * c
        return {"rank": z, "tiles": (xi * 4 + yi) * 2 + c}

    def devz(d):
        return {"rank": lax.rem(z + d + 4, 4), "tiles": t}

    sib = {"rank": z, "tiles": t + 1 - 2 * c}
    partners = (dev(f + 1, s), dev(f - 1, s), dev(f, s + 1), dev(f, s - 1), devz(1), devz(-1), sib)
    mask_copy = pltpu.make_async_copy(mask_hbm, mask, mask_sem)
    mask_copy.start()
    barrier = pltpu.get_barrier_semaphore()
    for p in partners:
        pl.semaphore_signal(barrier, inc=1, device_id=p, device_id_type=MESH)
    pl.semaphore_wait(barrier, len(partners))

    def rcopy(src, dst, ss, rs, to):
        return pltpu.make_async_remote_copy(
            src_ref=src, dst_ref=dst, send_sem=ss, recv_sem=rs, device_id=to, device_id_type=MESH
        )

    started = []

    def ag(k, start, size, to, src=None):
        view = items.at[pl.ds(start, size)]
        cp = rcopy(view if src is None else src, view, ag_send.at[k], ag_recv.at[k], to)
        cp.start()
        started.append(cp)

    def got(k, start, size):
        view = items.at[pl.ds(start, size)]
        rcopy(view, view, ag_send.at[k], ag_recv.at[k], sib).wait_recv()

    def blk(ci, si, fi):
        return ((ci * 4 + lax.rem(si + 4, 4)) * 4 + lax.rem(fi + 4, 4)) * 2

    ag(0, blk(c, s, f), 2, dev(f + 1, s), shard_ref)
    ag(1, blk(c, s, f), 2, dev(f - 1, s), shard_ref)
    items[pl.ds(blk(c, s, f), 2)] = shard_ref[...]
    got(0, blk(c, s, f - 1), 2)
    ag(2, blk(c, s, f - 1), 1, dev(f + 1, s))
    got(1, blk(c, s, f + 1), 2)
    ag(3, blk(c, s, f + 1) + 1, 1, dev(f - 1, s))
    got(2, blk(c, s, f + 2), 1)
    got(3, blk(c, s, f + 2) + 1, 1)
    slab = lambda si: blk(c, si, f * 0)
    other = lambda si: blk(1 - c, si, f * 0)
    ag(4, slab(s), 8, dev(f, s + 1))
    ag(5, slab(s), 8, dev(f, s - 1))
    ag(6, slab(s), 8, sib)
    got(4, slab(s - 1), 8)
    ag(7, slab(s - 1), 4, dev(f, s + 1))
    ag(8, slab(s - 1), 8, sib)
    got(5, slab(s + 1), 8)
    ag(9, slab(s + 1) + 4, 4, dev(f, s - 1))
    ag(10, slab(s + 1), 8, sib)
    got(7, slab(s + 2), 4)
    got(9, slab(s + 2) + 4, 4)
    ag(11, slab(s + 2), 8, sib)
    got(6, other(f), 8)
    got(8, other(f - 1), 8)
    got(10, other(f + 1), 8)
    got(11, other(f + 2), 8)
    mask_copy.wait()
    ugrad_ref[...] = jnp.zeros_like(ugrad_ref)
    run[...] = jnp.zeros_like(run)

    right, left = devz(1), devz(-1)

    def zcopies(ph, j):
        o = z
        if ph == 0:
            return (
                rcopy(send1.at[j, pl.ds(0, 2)], recv1.at[j, 0], z_send.at[ph, j, 0], z_recv.at[ph, j, 0], right),
                rcopy(send1.at[j, pl.ds(2, 2)], recv1.at[j, 1], z_send.at[ph, j, 1], z_recv.at[ph, j, 1], left),
            )
        if ph == 1:
            return (
                rcopy(send2.at[j, 0], recv2.at[j, 0], z_send.at[ph, j, 0], z_recv.at[ph, j, 0], right),
                rcopy(send2.at[j, 1], recv2.at[j, 1], z_send.at[ph, j, 1], z_recv.at[ph, j, 1], left),
            )
        if ph == 2:
            return (
                rcopy(resid.at[j, o], resid.at[j, o], z_send.at[ph, j, 0], z_recv.at[ph, j, 0], right),
                rcopy(resid.at[j, o], resid.at[j, o], z_send.at[ph, j, 1], z_recv.at[ph, j, 1], left),
            )
        lo, hi = lax.rem(z + 3, 4), lax.rem(z + 1, 4)
        a = resid.at[j, lo, pl.ds(0, 2)]
        b = resid.at[j, hi, pl.ds(2, 2)]
        return (
            rcopy(a, a, z_send.at[ph, j, 0], z_recv.at[ph, j, 0], right),
            rcopy(b, b, z_send.at[ph, j, 1], z_recv.at[ph, j, 1], left),
        )

    def zwait(ph, j):
        lo, hi, far = lax.rem(z + 3, 4), lax.rem(z + 1, 4), lax.rem(z + 2, 4)
        if ph == 0:
            views = (recv1.at[j, 0], recv1.at[j, 1])
        elif ph == 1:
            views = (recv2.at[j, 0], recv2.at[j, 1])
        elif ph == 2:
            views = (resid.at[j, lo], resid.at[j, hi])
        else:
            views = (resid.at[j, far, pl.ds(0, 2)], resid.at[j, far, pl.ds(2, 2)])
        for d in range(2):
            rcopy(views[d], views[d], z_send.at[ph, j, d], z_recv.at[ph, j, d], right).wait_recv()

    def item_context(p):
        it = items[place_ref[p]].astype(F32)
        return (it * crow_ref[pl.ds(p, 1), :]).astype(BF16)

    def predict(j):
        slot = lax.rem(j, 4)

        def tile(n, _):
            o, k = n // PER, lax.rem(n, PER)
            p = j * 16 + n
            pr = lax.dot_general(
                users_ref[user_ref[p]], item_context(p), (((1,), (1,)), ((), ())), preferred_element_type=F32
            )
            part[slot, o, k] = pr
            return 0

        lax.fori_loop(0, 16, tile, 0)
        send1[j] = part[slot, lax.rem(z + 2, 4)].astype(BF16)
        for cp in zcopies(0, j):
            cp.start()

    def combine(j):
        slot = lax.rem(j, 4)
        hi, lo = lax.rem(z + 1, 4), lax.rem(z + 3, 4)
        zwait(0, j)
        send2[j, 0, pl.ds(0, 2)] = (part[slot, hi, pl.ds(0, 2)] + recv1[j, 0].astype(F32)).astype(BF16)
        send2[j, 0, pl.ds(2, 2)] = part[slot, hi, pl.ds(2, 2)].astype(BF16)
        send2[j, 1, pl.ds(0, 2)] = part[slot, lo, pl.ds(0, 2)].astype(BF16)
        send2[j, 1, pl.ds(2, 2)] = (part[slot, lo, pl.ds(2, 2)] + recv1[j, 1].astype(F32)).astype(BF16)
        for cp in zcopies(1, j):
            cp.start()

    def weigh(j):
        slot = lax.rem(j, 4)
        zwait(1, j)
        for k in range(PER):
            p = j * 16 + z * PER + k
            pr = part[slot, z, k] + recv2[j, 0, k].astype(F32) + recv2[j, 1, k].astype(F32)
            m = mask[perm_ref[p]].astype(F32)
            resid[j, z, k] = (live_ref[p] * (1.0 + 4.0 * m) * (pr - m) * (1.0 / 128.0)).astype(BF16)
        for cp in zcopies(2, j):
            cp.start()

    def forward(j):
        zwait(2, j)
        for cp in zcopies(3, j):
            cp.start()

    def gradients(j):
        zwait(3, j)

        def group(o, _):
            for k in range(PER):
                p = j * 16 + o * PER + k
                r = resid[j, o, k]
                u = user_ref[p]
                for b in range(8):
                    ahot[pl.ds(b * SIDE, SIDE), pl.ds(k * SIDE, SIDE)] = jnp.where(u == b, r, jnp.zeros_like(r))
                it = items[place_ref[p]].astype(F32)
                cr = crow_ref[pl.ds(p, 1), :]
                icb[pl.ds(k * SIDE, SIDE), :] = (it * cr).astype(BF16)
                q = lax.dot_general(r, users_ref[u], (((0,), (0,)), ((), ())), preferred_element_type=F32)
                cterm_ref[pl.ds(p, 1), :] = jnp.sum(it * q, axis=0, keepdims=True)
                total = run[...] * keep_ref[p] + q * cr
                run[...] = total
                segs[p] = total.astype(BF16)
            ugrad_ref[...] += jnp.dot(ahot[...], icb[...], preferred_element_type=F32)
            return 0

        lax.fori_loop(0, 4, group, 0)

    def step(i, _):
        @pl.when(i < NB)
        def _():
            predict(i)

        @pl.when((i >= 1) & (i < NB + 1))
        def _():
            combine(i - 1)

        @pl.when((i >= 2) & (i < NB + 2))
        def _():
            weigh(i - 2)

        @pl.when((i >= 3) & (i < NB + 3))
        def _():
            forward(i - 3)

        @pl.when(i >= 4)
        def _():
            gradients(i - 4)

        return 0

    lax.fori_loop(0, NB + 4, step, 0)

    def finish(b, _):
        ipart_ref[b] = segs[last_ref[b]].astype(F32) * has_ref[b]
        return 0

    lax.fori_loop(0, 64, finish, 0)
    for cp in started:
        cp.wait_send()
    for ph in range(4):
        def drain(j, _):
            for cp in zcopies(ph, j):
                cp.wait_send()
            return 0

        lax.fori_loop(0, NB, drain, 0)


def local(
    user_factor,
    item_factor,
    context_factor,
    tile_user,
    tile_item,
    tile_context,
    tile_count,
    tile_mask,
    item_slot,
):
    n = tile_user.shape[0]
    nblocks = item_slot.shape[0]
    nctx = context_factor.shape[0]
    ids = jnp.arange(n, dtype=jnp.int32)
    hot_id = (tile_item[:, None] == jnp.arange(nblocks)[None, :]).astype(jnp.int32)
    slots = jnp.sum(hot_id * item_slot[None, :], axis=1)

    def place_of(block):
        owner, half = block // 2, block % 2
        core, xi, yi = owner % 2, owner // 8, (owner // 2) % 4
        fi = jnp.where(core == 0, xi, yi)
        si = jnp.where(core == 0, yi, xi)
        return ((core * 4 + si) * 4 + fi) * 2 + half

    place = place_of(slots)
    key = place * n + ids
    rank = jnp.sum((key[None, :] < key[:, None]).astype(jnp.int32), axis=1)
    pick = (rank[None, :] == ids[:, None]).astype(jnp.int32)
    live = (ids < tile_count[0]).astype(jnp.int32)
    vals = jnp.stack([place, tile_user, ids, live, tile_context])
    ordered = jnp.sum(pick[None] * vals[:, None, :], axis=2)
    place_s, user_s, perm, live_s, ctx_s = (ordered[i] for i in range(5))
    before = jnp.concatenate([jnp.full((1,), -1, jnp.int32), place_s[:-1]])
    keep = (place_s == before).astype(F32)
    ends = place_of(jnp.arange(nblocks, dtype=jnp.int32))
    last = jnp.maximum(jnp.sum((place[None, :] <= ends[:, None]).astype(jnp.int32), axis=1) - 1, 0)
    has = jnp.any(place[None, :] == ends[:, None], axis=1).astype(F32)
    chot = ctx_s[:, None] == jnp.arange(nctx)[None, :]
    crow = jnp.dot(chot.astype(BF16), context_factor, preferred_element_type=F32)
    smem = pl.BlockSpec(memory_space=pltpu.SMEM)
    vmem = pl.BlockSpec(memory_space=pltpu.VMEM)
    tile2 = (SIDE, SIDE)
    ugrad, ipart, cterm = pl.pallas_call(
        kernel,
        out_shape=(
            jax.ShapeDtypeStruct((1024, WIDTH), F32),
            jax.ShapeDtypeStruct((nblocks, SIDE, WIDTH), F32),
            jax.ShapeDtypeStruct((n, WIDTH), F32),
        ),
        in_specs=[smem] * 7 + [vmem] * 3 + [pl.BlockSpec(memory_space=pl.ANY)],
        out_specs=(vmem,) * 3,
        scratch_shapes=[
            pltpu.VMEM((64, SIDE, WIDTH), BF16),
            pltpu.VMEM((n,) + tile2, jnp.int32),
            pltpu.VMEM((4, 4, PER) + tile2, F32),
            pltpu.VMEM((NB, PER) + tile2, BF16),
            pltpu.VMEM((NB, 2, 2) + tile2, BF16),
            pltpu.VMEM((NB, 2, PER) + tile2, BF16),
            pltpu.VMEM((NB, 2, PER) + tile2, BF16),
            pltpu.VMEM((NB, 4, PER) + tile2, BF16),
            pltpu.VMEM((SIDE, WIDTH), F32),
            pltpu.VMEM((n, SIDE, WIDTH), BF16),
            pltpu.VMEM((1024, PER * SIDE), BF16),
            pltpu.VMEM((PER * SIDE, WIDTH), BF16),
            pltpu.SemaphoreType.DMA,
            pltpu.SemaphoreType.DMA((12,)),
            pltpu.SemaphoreType.DMA((12,)),
            pltpu.SemaphoreType.DMA((4, NB, 2)),
            pltpu.SemaphoreType.DMA((4, NB, 2)),
        ],
        compiler_params=pltpu.CompilerParams(
            collective_id=0, has_side_effects=True, vmem_limit_bytes=62 * 1024 * 1024
        ),
        cost_estimate=pl.CostEstimate(flops=10_000_000_000, bytes_accessed=20_000_000, transcendentals=0),
    )(
        place_s,
        user_s,
        perm,
        live_s.astype(F32),
        keep,
        last,
        has,
        user_factor.reshape(-1, SIDE, WIDTH),
        item_factor.reshape(-1, SIDE, WIDTH),
        crow,
        tile_mask,
    )
    item_grad = lax.psum_scatter(ipart, "tiles", scatter_dimension=0, tiled=True)
    ctx_part = jnp.dot(chot.astype(F32).T, cterm, precision=lax.Precision.HIGHEST)
    context_grad = lax.psum(ctx_part, "tiles")
    return (ugrad, item_grad.reshape(-1, WIDTH), context_grad)


def solution(mesh):
    return jax.shard_map(
        local,
        mesh=mesh,
        in_specs=(
            P("tiles", "rank"),
            P("tiles", "rank"),
            P(None, "rank"),
            P("tiles"),
            P("tiles"),
            P("tiles"),
            P("tiles"),
            P("tiles", None, None),
            P(),
        ),
        out_specs=(P("tiles", "rank"), P("tiles", "rank"), P(None, "rank")),
        check_vma=False,
    )
```

```python
import functools

import jax
import jax.numpy as jnp
from jax import lax
from jax.experimental import pallas as pl
from jax.experimental.pallas import tpu as pltpu
from jax.sharding import PartitionSpec as P

MESH = pl.DeviceIdType.MESH
BF16 = jnp.bfloat16
F32 = jnp.float32
NB = 8
PER = 4
SIDE = 128
WIDTH = 256
ROWS_A = 96
PLACE, USER, PERM, LIVE, CTXT, KEEP, LAST, HAS = range(8)


def kernel(
    meta_ref,
    users_ref,
    shard_ref,
    context_ref,
    ids_ref,
    mask_hbm,
    ugrad_ref,
    igrad_ref,
    cgrad_ref,
    items,
    mask,
    ctx32,
    part,
    send1,
    recv1,
    send2,
    recv2,
    resid,
    run,
    segs,
    ahot,
    icb,
    cterm,
    call,
    idall,
    chot,
    xs,
    xr,
    r1a,
    r1ra,
    r1b,
    r1rb,
    acc,
    r2a,
    r2ra,
    r2b,
    r2rb,
    mask_sem,
    ag_send,
    ag_recv,
    z_send,
    z_recv,
    c_send,
    c_recv,
    r_send,
    r_recv,
):
    z = lax.axis_index("rank")
    t = lax.axis_index("tiles")
    c = lax.rem(t, 2)
    y = lax.rem(t // 2, 4)
    x = t // 8
    f = x * (1 - c) + y * c
    s = y * (1 - c) + x * c

    def dev(fi, si):
        fi, si = lax.rem(fi + 4, 4), lax.rem(si + 4, 4)
        xi = fi * (1 - c) + si * c
        yi = si * (1 - c) + fi * c
        return {"rank": z, "tiles": (xi * 4 + yi) * 2 + c}

    def devz(d):
        return {"rank": lax.rem(z + d + 4, 4), "tiles": t}

    sib = {"rank": z, "tiles": t + 1 - 2 * c}
    partners = (dev(f + 1, s), dev(f - 1, s), dev(f, s + 1), dev(f, s - 1), devz(1), devz(-1), sib)
    mask_copy = pltpu.make_async_copy(mask_hbm, mask, mask_sem)
    mask_copy.start()
    barrier = pltpu.get_barrier_semaphore()
    for p in partners:
        pl.semaphore_signal(barrier, inc=1, device_id=p, device_id_type=MESH)
    pl.semaphore_wait(barrier, len(partners))

    def rcopy(src, dst, ss, rs, to):
        return pltpu.make_async_remote_copy(
            src_ref=src, dst_ref=dst, send_sem=ss, recv_sem=rs, device_id=to, device_id_type=MESH
        )

    started = []

    def ag(k, start, size, to, src=None):
        view = items.at[pl.ds(start, size)]
        cp = rcopy(view if src is None else src, view, ag_send.at[k], ag_recv.at[k], to)
        cp.start()
        started.append(cp)

    def got(k, start, size):
        view = items.at[pl.ds(start, size)]
        rcopy(view, view, ag_send.at[k], ag_recv.at[k], sib).wait_recv()

    def blk(ci, si, fi):
        return ((ci * 4 + lax.rem(si + 4, 4)) * 4 + lax.rem(fi + 4, 4)) * 2

    ag(0, blk(c, s, f), 2, dev(f + 1, s), shard_ref)
    ag(1, blk(c, s, f), 2, dev(f - 1, s), shard_ref)
    items[pl.ds(blk(c, s, f), 2)] = shard_ref[...]
    ctx32[...] = context_ref[...].astype(F32)
    got(0, blk(c, s, f - 1), 2)
    ag(2, blk(c, s, f - 1), 1, dev(f + 1, s))
    got(1, blk(c, s, f + 1), 2)
    ag(3, blk(c, s, f + 1) + 1, 1, dev(f - 1, s))
    got(2, blk(c, s, f + 2), 1)
    got(3, blk(c, s, f + 2) + 1, 1)
    slab = lambda si: blk(c, si, f * 0)
    other = lambda si: blk(1 - c, si, f * 0)
    ag(4, slab(s), 8, dev(f, s + 1))
    ag(5, slab(s), 8, dev(f, s - 1))
    ag(6, slab(s), 8, sib)
    got(4, slab(s - 1), 8)
    ag(7, slab(s - 1), 4, dev(f, s + 1))
    ag(8, slab(s - 1), 8, sib)
    got(5, slab(s + 1), 8)
    ag(9, slab(s + 1) + 4, 4, dev(f, s - 1))
    ag(10, slab(s + 1), 8, sib)
    got(7, slab(s + 2), 4)
    got(9, slab(s + 2) + 4, 4)
    ag(11, slab(s + 2), 8, sib)
    got(6, other(f), 8)
    got(8, other(f - 1), 8)
    got(10, other(f + 1), 8)
    got(11, other(f + 2), 8)
    mask_copy.wait()
    ugrad_ref[...] = jnp.zeros_like(ugrad_ref)
    run[...] = jnp.zeros_like(run)

    right, left = devz(1), devz(-1)

    def zcopies(ph, j):
        o = z
        if ph == 0:
            return (
                rcopy(send1.at[j, pl.ds(0, 2)], recv1.at[j, 0], z_send.at[ph, j, 0], z_recv.at[ph, j, 0], right),
                rcopy(send1.at[j, pl.ds(2, 2)], recv1.at[j, 1], z_send.at[ph, j, 1], z_recv.at[ph, j, 1], left),
            )
        if ph == 1:
            return (
                rcopy(send2.at[j, 0], recv2.at[j, 0], z_send.at[ph, j, 0], z_recv.at[ph, j, 0], right),
                rcopy(send2.at[j, 1], recv2.at[j, 1], z_send.at[ph, j, 1], z_recv.at[ph, j, 1], left),
            )
        if ph == 2:
            return (
                rcopy(resid.at[j, o], resid.at[j, o], z_send.at[ph, j, 0], z_recv.at[ph, j, 0], right),
                rcopy(resid.at[j, o], resid.at[j, o], z_send.at[ph, j, 1], z_recv.at[ph, j, 1], left),
            )
        lo, hi = lax.rem(z + 3, 4), lax.rem(z + 1, 4)
        a = resid.at[j, lo, pl.ds(0, 2)]
        b = resid.at[j, hi, pl.ds(2, 2)]
        return (
            rcopy(a, a, z_send.at[ph, j, 0], z_recv.at[ph, j, 0], right),
            rcopy(b, b, z_send.at[ph, j, 1], z_recv.at[ph, j, 1], left),
        )

    def zwait(ph, j):
        lo, hi, far = lax.rem(z + 3, 4), lax.rem(z + 1, 4), lax.rem(z + 2, 4)
        if ph == 0:
            views = (recv1.at[j, 0], recv1.at[j, 1])
        elif ph == 1:
            views = (recv2.at[j, 0], recv2.at[j, 1])
        elif ph == 2:
            views = (resid.at[j, lo], resid.at[j, hi])
        else:
            views = (resid.at[j, far, pl.ds(0, 2)], resid.at[j, far, pl.ds(2, 2)])
        for d in range(2):
            rcopy(views[d], views[d], z_send.at[ph, j, d], z_recv.at[ph, j, d], right).wait_recv()

    def item_context(p):
        it = items[meta_ref[PLACE, p]].astype(F32)
        return (it * ctx32[pl.ds(meta_ref[CTXT, p], 1), :]).astype(BF16)

    def predict(j):
        slot = lax.rem(j, 4)

        def tile(n, _):
            o, k = n // PER, lax.rem(n, PER)
            p = j * 16 + n
            pr = lax.dot_general(
                users_ref[meta_ref[USER, p]], item_context(p), (((1,), (1,)), ((), ())), preferred_element_type=F32
            )
            part[slot, o, k] = pr
            return 0

        lax.fori_loop(0, 16, tile, 0)
        send1[j] = part[slot, lax.rem(z + 2, 4)].astype(BF16)
        for cp in zcopies(0, j):
            cp.start()

    def combine(j):
        slot = lax.rem(j, 4)
        hi, lo = lax.rem(z + 1, 4), lax.rem(z + 3, 4)
        zwait(0, j)
        send2[j, 0, pl.ds(0, 2)] = (part[slot, hi, pl.ds(0, 2)] + recv1[j, 0].astype(F32)).astype(BF16)
        send2[j, 0, pl.ds(2, 2)] = part[slot, hi, pl.ds(2, 2)].astype(BF16)
        send2[j, 1, pl.ds(0, 2)] = part[slot, lo, pl.ds(0, 2)].astype(BF16)
        send2[j, 1, pl.ds(2, 2)] = (part[slot, lo, pl.ds(2, 2)] + recv1[j, 1].astype(F32)).astype(BF16)
        for cp in zcopies(1, j):
            cp.start()

    def weigh(j):
        slot = lax.rem(j, 4)
        zwait(1, j)
        for k in range(PER):
            p = j * 16 + z * PER + k
            pr = part[slot, z, k] + recv2[j, 0, k].astype(F32) + recv2[j, 1, k].astype(F32)
            m = mask[meta_ref[PERM, p]].astype(F32)
            resid[j, z, k] = (meta_ref[LIVE, p].astype(F32) * (1.0 + 4.0 * m) * (pr - m) * (1.0 / 128.0)).astype(BF16)
        for cp in zcopies(2, j):
            cp.start()

    def forward(j):
        zwait(2, j)
        for cp in zcopies(3, j):
            cp.start()

    def gradients(j):
        zwait(3, j)

        def group(o, _):
            for k in range(PER):
                p = j * 16 + o * PER + k
                r = resid[j, o, k]
                u = meta_ref[USER, p]
                for b in range(8):
                    ahot[pl.ds(b * SIDE, SIDE), pl.ds(k * SIDE, SIDE)] = jnp.where(u == b, r, jnp.zeros_like(r))
                it = items[meta_ref[PLACE, p]].astype(F32)
                cr = ctx32[pl.ds(meta_ref[CTXT, p], 1), :]
                icb[pl.ds(k * SIDE, SIDE), :] = (it * cr).astype(BF16)
                q = lax.dot_general(r, users_ref[u], (((0,), (0,)), ((), ())), preferred_element_type=F32)
                cterm[pl.ds(p, 1), :] = jnp.sum(it * q, axis=0, keepdims=True)
                total = run[...] * meta_ref[KEEP, p].astype(F32) + q * cr
                run[...] = total
                segs[p] = total.astype(BF16)
            ugrad_ref[...] += jnp.dot(ahot[...], icb[...], preferred_element_type=F32)
            return 0

        lax.fori_loop(0, 4, group, 0)

    def ccopies(g, k, arriving):
        rows = pl.ds(0, ROWS_A) if g == 0 else pl.ds(ROWS_A, SIDE - ROWS_A)
        pos = lambda ci, si, fi: (ci * 4 + lax.rem(si + 4, 4)) * 4 + lax.rem(fi + 4, 4)
        start, count, to = (
            (pos(c, s, f), 1, dev(f + 1, s)),
            (pos(c, s, f), 1, dev(f - 1, s)),
            (pos(c, s, f - 1), 1, dev(f + 1, s)),
            (pos(c, s, 0 * f), 4, dev(f, s + 1)),
            (pos(c, s, 0 * f), 4, dev(f, s - 1)),
            (pos(c, s - 1, 0 * f), 4, dev(f, s + 1)),
            (c * 16, 16, sib),
        )[k]
        into = (
            pos(c, s, f - 1),
            pos(c, s, f + 1),
            pos(c, s, f + 2),
            pos(c, s - 1, 0 * f),
            pos(c, s + 1, 0 * f),
            pos(c, s + 2, 0 * f),
            (1 - c) * 16,
        )[k]
        at = into if arriving else start
        views = [(call.at[pl.ds(at, count), rows], g)]
        if g == 0:
            views.append((idall.at[pl.ds(at, count)], 2))
        return [rcopy(a, a, c_send.at[h, k], c_recv.at[h, k], to) for a, h in views]

    def cstart(g, k):
        for cp in ccopies(g, k, False):
            cp.start()

    def cwait(g, k):
        for cp in ccopies(g, k, True):
            cp.wait_recv()

    def tick(g, n):
        if n == 0:
            own = (c * 4 + s) * 4 + f
            if g == 0:
                call[own, pl.ds(0, ROWS_A)] = cterm[pl.ds(0, ROWS_A), :].astype(BF16)
                idall[own] = ids_ref[...]
            else:
                call[own, pl.ds(ROWS_A, SIDE - ROWS_A)] = cterm[pl.ds(ROWS_A, SIDE - ROWS_A), :].astype(BF16)
            cstart(g, 0)
            cstart(g, 1)
        elif n == 1:
            cwait(g, 0)
            cstart(g, 2)
            cwait(g, 1)
        elif n == 2:
            cwait(g, 2)
            cstart(g, 3)
            cstart(g, 4)
        elif n == 3:
            cwait(g, 3)
            cstart(g, 5)
            cwait(g, 4)
        elif n == 4:
            cwait(g, 5)
            cstart(g, 6)
        else:
            cwait(g, 6)

    def step(i, _):
        @pl.when(i == NB + 2)
        def _():
            tick(0, 1)

        @pl.when(i == NB + 3)
        def _():
            tick(0, 3)

        @pl.when(i < NB)
        def _():
            predict(i)

        @pl.when((i >= 1) & (i < NB + 1))
        def _():
            combine(i - 1)

        @pl.when((i >= 2) & (i < NB + 2))
        def _():
            weigh(i - 2)

        @pl.when((i >= 3) & (i < NB + 3))
        def _():
            forward(i - 3)

        @pl.when(i >= 4)
        def _():
            gradients(i - 4)

        @pl.when(i == NB + 1)
        def _():
            tick(0, 0)

        @pl.when(i == NB + 2)
        def _():
            tick(0, 2)

        @pl.when(i == NB + 3)
        def _():
            tick(0, 4)

        return 0

    lax.fori_loop(0, NB + 4, step, 0)

    def rc(k, src, dst, to):
        return rcopy(src, dst, r_send.at[k], r_recv.at[k], to)

    def rgot(k, dst):
        rc(k, dst, dst, sib).wait_recv()

    def own_sum(b):
        return segs[meta_ref[LAST, b]].astype(F32) * meta_ref[HAS, b].astype(F32)

    rcs = []

    def rstart(k, src, dst, to):
        cp = rc(k, src, dst, to)
        cp.start()
        rcs.append(cp)

    for k, d in enumerate((2, 1, 3, 0)):
        theirs = lax.rem(f + d, 4) * 8

        def give(n, _):
            xs[theirs + n] = own_sum((1 - c) * 32 + theirs + n).astype(BF16)
            return 0

        lax.fori_loop(0, 8, give, 0)
        piece = pl.ds(theirs, 8)
        rstart(k, xs.at[piece], xr.at[piece], sib)
        if k == 0:
            tick(1, 0)
    tick(0, 5)

    def hots(n, _):
        ids = idall[n][0:1, :].astype(F32)
        rows = lax.broadcasted_iota(jnp.int32, (WIDTH, SIDE), 0).astype(F32)
        chot[n] = jnp.where(rows == ids, 1.0, 0.0).astype(BF16)
        return 0

    lax.fori_loop(0, 32, hots, 0)

    def chip_sum(si, n):
        return own_sum(c * 32 + si * 8 + n) + xr[si * 8 + n].astype(F32)

    def each(lo, hi, body):
        def run_body(n, _):
            body(n)
            return 0

        lax.fori_loop(lo, hi, run_body, 0)

    far, hi, lo = lax.rem(s + 2, 4), lax.rem(s + 1, 4), lax.rem(s + 3, 4)
    ahead, behind = dev(f, s + 1), dev(f, s - 1)

    def put_far(n):
        r1a[n] = chip_sum(far, n).astype(BF16)

    rgot(0, xr.at[pl.ds(far * 8, 8)])
    each(0, 8, put_far)
    rstart(4, r1a.at[pl.ds(0, 4)], r1ra.at[0], ahead)
    rstart(5, r1a.at[pl.ds(4, 4)], r1ra.at[1], behind)
    tick(1, 1)

    def put_hi(n):
        r1b[0, n] = chip_sum(hi, n).astype(BF16)

    def put_hi_more(n):
        r1b[0, n] = (chip_sum(hi, n) + r1ra[0, n].astype(F32)).astype(BF16)

    def put_lo(n):
        r1b[1, n] = chip_sum(lo, n).astype(BF16)

    def put_lo_more(n):
        r1b[1, n] = (chip_sum(lo, n) + r1ra[1, n - 4].astype(F32)).astype(BF16)

    rgot(1, xr.at[pl.ds(hi * 8, 8)])
    each(4, 8, put_hi)
    rgot(2, xr.at[pl.ds(lo * 8, 8)])
    each(0, 4, put_lo)
    rgot(4, r1ra.at[0])
    each(0, 4, put_hi_more)
    rstart(6, r1b.at[0], r1rb.at[0], ahead)
    rgot(5, r1ra.at[1])
    each(4, 8, put_lo_more)
    rstart(7, r1b.at[1], r1rb.at[1], behind)
    tick(1, 2)

    def put_mine(n):
        acc[n] = chip_sum(s, n)

    def put_mine_more(n):
        acc[n] += r1rb[0, n].astype(F32) + r1rb[1, n].astype(F32)

    rgot(3, xr.at[pl.ds(s * 8, 8)])
    each(0, 8, put_mine)
    rgot(6, r1rb.at[0])
    rgot(7, r1rb.at[1])
    each(0, 8, put_mine_more)

    far, hi, lo = lax.rem(f + 2, 4) * 2, lax.rem(f + 1, 4) * 2, lax.rem(f + 3, 4) * 2
    ahead, behind = dev(f + 1, s), dev(f - 1, s)
    r2a[...] = acc[pl.ds(far, 2)].astype(BF16)
    rstart(8, r2a.at[0], r2ra.at[0], ahead)
    rstart(9, r2a.at[1], r2ra.at[1], behind)
    tick(1, 3)
    r2b[0, 1] = acc[hi + 1].astype(BF16)
    r2b[1, 0] = acc[lo].astype(BF16)
    rgot(8, r2ra.at[0])
    r2b[0, 0] = (acc[hi] + r2ra[0].astype(F32)).astype(BF16)
    rstart(10, r2b.at[0], r2rb.at[0], ahead)
    rgot(9, r2ra.at[1])
    r2b[1, 1] = (acc[lo + 1] + r2ra[1].astype(F32)).astype(BF16)
    rstart(11, r2b.at[1], r2rb.at[1], behind)
    tick(1, 4)
    rgot(10, r2rb.at[0])
    rgot(11, r2rb.at[1])
    igrad_ref[...] = acc[pl.ds(f * 2, 2)] + r2rb[0].astype(F32) + r2rb[1].astype(F32)
    tick(1, 5)
    cgrad_ref[...] = jnp.zeros_like(cgrad_ref)

    def ctx_dot(n):
        cgrad_ref[...] += jnp.dot(chot[n], call[n], preferred_element_type=F32)

    each(0, 32, ctx_dot)

    for cp in started + rcs:
        cp.wait_send()
    for g in range(2):
        for k in range(7):
            for cp in ccopies(g, k, False):
                cp.wait_send()
    for ph in range(4):
        def drain(j, _):
            for cp in zcopies(ph, j):
                cp.wait_send()
            return 0

        lax.fori_loop(0, NB, drain, 0)


def local(
    user_factor,
    item_factor,
    context_factor,
    tile_user,
    tile_item,
    tile_context,
    tile_count,
    tile_mask,
    item_slot,
):
    n = tile_user.shape[0]
    nblocks = item_slot.shape[0]
    nctx = context_factor.shape[0]
    ids = jnp.arange(n, dtype=jnp.int32)
    hot_id = (tile_item[:, None] == jnp.arange(nblocks)[None, :]).astype(jnp.int32)
    slots = jnp.sum(hot_id * item_slot[None, :], axis=1)

    def place_of(block):
        owner, half = block // 2, block % 2
        core, xi, yi = owner % 2, owner // 8, (owner // 2) % 4
        fi = jnp.where(core == 0, xi, yi)
        si = jnp.where(core == 0, yi, xi)
        return ((core * 4 + si) * 4 + fi) * 2 + half

    place = place_of(slots)
    key = place * n + ids
    rank = jnp.sum((key[None, :] < key[:, None]).astype(jnp.int32), axis=1)
    pick = (rank[None, :] == ids[:, None]).astype(jnp.int32)
    live = (ids < tile_count[0]).astype(jnp.int32)
    vals = jnp.stack([place, tile_user, ids, live, tile_context])
    ordered = jnp.sum(pick[None] * vals[:, None, :], axis=2)
    place_s, ctx_s = ordered[PLACE], ordered[CTXT]
    before = jnp.concatenate([jnp.full((1,), -1, jnp.int32), place_s[:-1]])
    keep = (place_s == before).astype(jnp.int32)
    last = jnp.maximum(jnp.sum((place[None, :] <= ids[:, None]).astype(jnp.int32), axis=1) - 1, 0)
    has = jnp.any(place[None, :] == ids[:, None], axis=1).astype(jnp.int32)
    meta = jnp.concatenate([ordered, jnp.stack([keep, last, has])])
    ids16 = jnp.broadcast_to(ctx_s.astype(BF16)[None, :], (16, n))
    smem = pl.BlockSpec(memory_space=pltpu.SMEM)
    vmem = pl.BlockSpec(memory_space=pltpu.VMEM)
    tile2 = (SIDE, SIDE)
    wide = (SIDE, WIDTH)
    ugrad, igrad, cgrad = pl.pallas_call(
        kernel,
        out_shape=(
            jax.ShapeDtypeStruct((1024, WIDTH), F32),
            jax.ShapeDtypeStruct((2,) + wide, F32),
            jax.ShapeDtypeStruct((nctx, WIDTH), F32),
        ),
        in_specs=[smem] + [vmem] * 4 + [pl.BlockSpec(memory_space=pl.ANY)],
        out_specs=(vmem,) * 3,
        scratch_shapes=[
            pltpu.VMEM((64,) + wide, BF16),
            pltpu.VMEM((n,) + tile2, jnp.int32),
            pltpu.VMEM((nctx, WIDTH), F32),
            pltpu.VMEM((4, 4, PER) + tile2, F32),
            pltpu.VMEM((NB, PER) + tile2, BF16),
            pltpu.VMEM((NB, 2, 2) + tile2, BF16),
            pltpu.VMEM((NB, 2, PER) + tile2, BF16),
            pltpu.VMEM((NB, 2, PER) + tile2, BF16),
            pltpu.VMEM((NB, 4, PER) + tile2, BF16),
            pltpu.VMEM(wide, F32),
            pltpu.VMEM((n,) + wide, BF16),
            pltpu.VMEM((1024, PER * SIDE), BF16),
            pltpu.VMEM((PER * SIDE, WIDTH), BF16),
            pltpu.VMEM(wide, F32),
            pltpu.VMEM((32,) + wide, BF16),
            pltpu.VMEM((32, 16, SIDE), BF16),
            pltpu.VMEM((32, nctx, SIDE), BF16),
            pltpu.VMEM((32,) + wide, BF16),
            pltpu.VMEM((32,) + wide, BF16),
            pltpu.VMEM((8,) + wide, BF16),
            pltpu.VMEM((2, 4) + wide, BF16),
            pltpu.VMEM((2, 8) + wide, BF16),
            pltpu.VMEM((2, 8) + wide, BF16),
            pltpu.VMEM((8,) + wide, F32),
            pltpu.VMEM((2,) + wide, BF16),
            pltpu.VMEM((2,) + wide, BF16),
            pltpu.VMEM((2, 2) + wide, BF16),
            pltpu.VMEM((2, 2) + wide, BF16),
            pltpu.SemaphoreType.DMA,
            pltpu.SemaphoreType.DMA((12,)),
            pltpu.SemaphoreType.DMA((12,)),
            pltpu.SemaphoreType.DMA((4, NB, 2)),
            pltpu.SemaphoreType.DMA((4, NB, 2)),
            pltpu.SemaphoreType.DMA((3, 7)),
            pltpu.SemaphoreType.DMA((3, 7)),
            pltpu.SemaphoreType.DMA((12,)),
            pltpu.SemaphoreType.DMA((12,)),
        ],
        compiler_params=pltpu.CompilerParams(
            collective_id=0, has_side_effects=True, vmem_limit_bytes=62 * 1024 * 1024
        ),
        cost_estimate=pl.CostEstimate(flops=10_000_000_000, bytes_accessed=20_000_000, transcendentals=0),
    )(
        meta,
        user_factor.reshape(-1, SIDE, WIDTH),
        item_factor.reshape(-1, SIDE, WIDTH),
        context_factor,
        ids16,
        tile_mask,
    )
    return (ugrad, igrad.reshape(-1, WIDTH), cgrad)


def solution(mesh):
    return jax.shard_map(
        local,
        mesh=mesh,
        in_specs=(
            P("tiles", "rank"),
            P("tiles", "rank"),
            P(None, "rank"),
            P("tiles"),
            P("tiles"),
            P("tiles"),
            P("tiles"),
            P("tiles", None, None),
            P(),
        ),
        out_specs=(P("tiles", "rank"), P("tiles", "rank"), P(None, "rank")),
        check_vma=False,
    )
```

```python
import functools

import jax
import jax.numpy as jnp
from jax import lax
from jax.experimental import pallas as pl
from jax.experimental.pallas import tpu as pltpu
from jax.sharding import PartitionSpec as P

MESH = pl.DeviceIdType.MESH
BF16 = jnp.bfloat16
F32 = jnp.float32
NB = 8
PER = 4
SIDE = 128
WIDTH = 256
ROWS_B = 32
ROWS_A = SIDE - ROWS_B
PLACE, USER, PERM, LIVE, CTXT, KEEP, LAST, HAS = range(8)


def kernel(
    meta_ref,
    users_ref,
    shard_ref,
    context_ref,
    ids_ref,
    mask_hbm,
    ugrad_ref,
    igrad_ref,
    cgrad_ref,
    items,
    mask,
    ctx32,
    part,
    send1,
    recv1,
    send2,
    recv2,
    resid,
    run,
    segs,
    ahot,
    icb,
    cterm,
    call_a,
    call_b,
    idall,
    chot_a,
    chot_b,
    xs,
    xr,
    r1s,
    r1r,
    r2s,
    r2r,
    mask_sem,
    ag_send,
    ag_recv,
    z_send,
    z_recv,
    c_send,
    c_recv,
    r_send,
    r_recv,
):
    z = lax.axis_index("rank")
    t = lax.axis_index("tiles")
    c = lax.rem(t, 2)
    y = lax.rem(t // 2, 4)
    x = t // 8
    f = x * (1 - c) + y * c
    s = y * (1 - c) + x * c

    def dev(fi, si):
        fi, si = lax.rem(fi + 4, 4), lax.rem(si + 4, 4)
        xi = fi * (1 - c) + si * c
        yi = si * (1 - c) + fi * c
        return {"rank": z, "tiles": (xi * 4 + yi) * 2 + c}

    def devz(d):
        return {"rank": lax.rem(z + d + 4, 4), "tiles": t}

    sib = {"rank": z, "tiles": t + 1 - 2 * c}
    turns = (1, 3, 2)
    fpeer = {d: dev(f + d, s) for d in turns}
    speer = {d: dev(f, s + d) for d in turns}
    partners = tuple(fpeer.values()) + tuple(speer.values()) + (devz(1), devz(-1), sib)
    mask_copy = pltpu.make_async_copy(mask_hbm, mask, mask_sem)
    mask_copy.start()
    barrier = pltpu.get_barrier_semaphore()
    for p in partners:
        pl.semaphore_signal(barrier, inc=1, device_id=p, device_id_type=MESH)
    pl.semaphore_wait(barrier, len(partners))

    def rcopy(src, dst, ss, rs, to):
        return pltpu.make_async_remote_copy(
            src_ref=src, dst_ref=dst, send_sem=ss, recv_sem=rs, device_id=to, device_id_type=MESH
        )

    started = []

    def blk(ci, si, fi):
        return ((ci * 4 + lax.rem(si + 4, 4)) * 4 + lax.rem(fi + 4, 4)) * 2

    def ag(k, start, size, to, src=None):
        view = items.at[pl.ds(start, size)]
        cp = rcopy(view if src is None else src, view, ag_send.at[k], ag_recv.at[k], to)
        cp.start()
        started.append(cp)

    def got(k, start, size):
        view = items.at[pl.ds(start, size)]
        rcopy(view, view, ag_send.at[k], ag_recv.at[k], sib).wait_recv()

    mine = blk(c, s, f)
    for d in turns:
        ag(d, mine, 2, fpeer[d], shard_ref)
    for d in turns:
        ag(4 + d, mine, 2, speer[d], shard_ref)
    items[pl.ds(mine, 2)] = shard_ref[...]
    ctx32[...] = context_ref[...].astype(F32)
    ugrad_ref[...] = jnp.zeros_like(ugrad_ref)
    run[...] = jnp.zeros_like(run)
    call_a[...] = jnp.zeros_like(call_a)
    for d in turns:
        e = 4 - d
        got(d, blk(c, s, f + e), 2)
        for dd in turns:
            ag(4 + 4 * e + dd, blk(c, s, f + e), 2, speer[dd])
    ag(20, blk(c, s, 0 * f), 8, sib)
    for d in turns:
        for e in (0, 3, 1, 2):
            got(4 + 4 * e + d, blk(c, s - d, f + e), 2)
        ag(20 + d, blk(c, s - d, 0 * f), 8, sib)
    for d in (0, 1, 3, 2):
        got(20 + d, blk(1 - c, f - d, 0 * f), 8)
    mask_copy.wait()

    right, left = devz(1), devz(-1)

    def zcopies(ph, j):
        o = z
        if ph == 0:
            return (
                rcopy(send1.at[j, pl.ds(0, 2)], recv1.at[j, 0], z_send.at[ph, j, 0], z_recv.at[ph, j, 0], right),
                rcopy(send1.at[j, pl.ds(2, 2)], recv1.at[j, 1], z_send.at[ph, j, 1], z_recv.at[ph, j, 1], left),
            )
        if ph == 1:
            return (
                rcopy(send2.at[j, 0], recv2.at[j, 0], z_send.at[ph, j, 0], z_recv.at[ph, j, 0], right),
                rcopy(send2.at[j, 1], recv2.at[j, 1], z_send.at[ph, j, 1], z_recv.at[ph, j, 1], left),
            )
        if ph == 2:
            return (
                rcopy(resid.at[j, o], resid.at[j, o], z_send.at[ph, j, 0], z_recv.at[ph, j, 0], right),
                rcopy(resid.at[j, o], resid.at[j, o], z_send.at[ph, j, 1], z_recv.at[ph, j, 1], left),
            )
        lo, hi = lax.rem(z + 3, 4), lax.rem(z + 1, 4)
        a = resid.at[j, lo, pl.ds(0, 2)]
        b = resid.at[j, hi, pl.ds(2, 2)]
        return (
            rcopy(a, a, z_send.at[ph, j, 0], z_recv.at[ph, j, 0], right),
            rcopy(b, b, z_send.at[ph, j, 1], z_recv.at[ph, j, 1], left),
        )

    def zwait(ph, j):
        lo, hi, far = lax.rem(z + 3, 4), lax.rem(z + 1, 4), lax.rem(z + 2, 4)
        if ph == 0:
            views = (recv1.at[j, 0], recv1.at[j, 1])
        elif ph == 1:
            views = (recv2.at[j, 0], recv2.at[j, 1])
        elif ph == 2:
            views = (resid.at[j, lo], resid.at[j, hi])
        else:
            views = (resid.at[j, far, pl.ds(0, 2)], resid.at[j, far, pl.ds(2, 2)])
        for d in range(2):
            rcopy(views[d], views[d], z_send.at[ph, j, d], z_recv.at[ph, j, d], right).wait_recv()

    def item_context(p):
        it = items[meta_ref[PLACE, p]].astype(F32)
        return (it * ctx32[pl.ds(meta_ref[CTXT, p], 1), :]).astype(BF16)

    def predict(j):
        slot = lax.rem(j, 4)

        def tile(n, _):
            o, k = n // PER, lax.rem(n, PER)
            p = j * 16 + n
            pr = lax.dot_general(
                users_ref[meta_ref[USER, p]], item_context(p), (((1,), (1,)), ((), ())), preferred_element_type=F32
            )
            part[slot, o, k] = pr
            return 0

        lax.fori_loop(0, 16, tile, 0)
        send1[j] = part[slot, lax.rem(z + 2, 4)].astype(BF16)
        for cp in zcopies(0, j):
            cp.start()

    def combine(j):
        slot = lax.rem(j, 4)
        hi, lo = lax.rem(z + 1, 4), lax.rem(z + 3, 4)
        zwait(0, j)
        send2[j, 0, pl.ds(0, 2)] = (part[slot, hi, pl.ds(0, 2)] + recv1[j, 0].astype(F32)).astype(BF16)
        send2[j, 0, pl.ds(2, 2)] = part[slot, hi, pl.ds(2, 2)].astype(BF16)
        send2[j, 1, pl.ds(0, 2)] = part[slot, lo, pl.ds(0, 2)].astype(BF16)
        send2[j, 1, pl.ds(2, 2)] = (part[slot, lo, pl.ds(2, 2)] + recv1[j, 1].astype(F32)).astype(BF16)
        for cp in zcopies(1, j):
            cp.start()

    def weigh(j):
        slot = lax.rem(j, 4)
        zwait(1, j)
        for k in range(PER):
            p = j * 16 + z * PER + k
            pr = part[slot, z, k] + recv2[j, 0, k].astype(F32) + recv2[j, 1, k].astype(F32)
            m = mask[meta_ref[PERM, p]].astype(F32)
            resid[j, z, k] = (meta_ref[LIVE, p].astype(F32) * (1.0 + 4.0 * m) * (pr - m) * (1.0 / 128.0)).astype(BF16)
        for cp in zcopies(2, j):
            cp.start()

    def forward(j):
        zwait(2, j)
        for cp in zcopies(3, j):
            cp.start()

    def gradients(j):
        zwait(3, j)

        def group(o, _):
            for k in range(PER):
                p = j * 16 + o * PER + k
                r = resid[j, o, k]
                u = meta_ref[USER, p]
                for b in range(8):
                    ahot[pl.ds(b * SIDE, SIDE), pl.ds(k * SIDE, SIDE)] = jnp.where(u == b, r, jnp.zeros_like(r))
                it = items[meta_ref[PLACE, p]].astype(F32)
                cr = ctx32[pl.ds(meta_ref[CTXT, p], 1), :]
                icb[pl.ds(k * SIDE, SIDE), :] = (it * cr).astype(BF16)
                q = lax.dot_general(r, users_ref[u], (((0,), (0,)), ((), ())), preferred_element_type=F32)
                cterm[pl.ds(p, 1), :] = jnp.sum(it * q, axis=0, keepdims=True)
                total = run[...] * meta_ref[KEEP, p].astype(F32) + q * cr
                run[...] = total
                segs[p] = total.astype(BF16)
            ugrad_ref[...] += jnp.dot(ahot[...], icb[...], preferred_element_type=F32)
            return 0

        lax.fori_loop(0, 4, group, 0)

    def ccopies(g, k, arriving):
        pos = lambda si, fi: (c * 4 + lax.rem(si + 4, 4)) * 4 + lax.rem(fi + 4, 4)
        if k < 4:
            at, count, to = (pos(s, f - k) if arriving else pos(s, f)), 1, fpeer[k]
        elif k < 8:
            at, count, to = (pos(s - (k - 4), 0 * f) if arriving else pos(s, 0 * f)), 4, speer[k - 4]
        else:
            at, count, to = ((1 - c) * 16 if arriving else c * 16), 16, sib
        if g == 0:
            a = call_a.at[pl.ds(at, count), pl.ds(0, ROWS_A)]
        else:
            a = (call_b if g == 1 else idall).at[pl.ds(at, count)]
        return rcopy(a, a, c_send.at[g, k], c_recv.at[g, k], to)

    def tick(g, n):
        own = (c * 4 + s) * 4 + f
        if n == 0:
            if g == 0:
                call_a[own, pl.ds(0, ROWS_A)] = cterm[pl.ds(0, ROWS_A), :].astype(BF16)
            elif g == 1:
                call_b[own] = cterm[pl.ds(ROWS_A, ROWS_B), :].astype(BF16)
            else:
                row = lax.broadcasted_iota(jnp.int32, (16, SIDE), 0)
                lane = lax.broadcasted_iota(jnp.int32, (16, SIDE), 1)
                hidden = (row == 1) & (lane // ROWS_B != f)
                idall[own] = jnp.where(hidden, 0.0, ids_ref[...].astype(F32)).astype(BF16)
        else:
            for d in turns if n < 3 else (0,):
                ccopies(g, 4 * (n - 1) + d, True).wait_recv()
        if n < 3:
            for d in turns if n < 2 else (0,):
                ccopies(g, 4 * n + d, False).start()

    def hot(ids):
        rows = lax.broadcasted_iota(jnp.int32, (WIDTH, SIDE), 0).astype(F32)
        return jnp.where(rows == ids, 1.0, 0.0).astype(BF16)

    def hots(n, _):
        rest = jnp.zeros((1, SIDE), F32)
        for k in range(4):
            both = idall[n * 4 + k].astype(F32)
            chot_a[n * 4 + k] = hot(both[0:1, :])
            rest += both[1:2, :]
        chot_b[n] = hot(rest)
        return 0

    def step(i, _):
        for n in range(4):

            @pl.when(i == 2 + n)
            def _():
                tick(2, n)

        @pl.when(i == NB + 3)
        def _():
            tick(0, 2)

        @pl.when(i < NB)
        def _():
            predict(i)

        @pl.when((i >= 1) & (i < NB + 1))
        def _():
            combine(i - 1)

        @pl.when((i >= 2) & (i < NB + 2))
        def _():
            weigh(i - 2)

        @pl.when((i >= 3) & (i < NB + 3))
        def _():
            forward(i - 3)

        @pl.when(i >= 4)
        def _():
            gradients(i - 4)

        @pl.when(i == NB + 1)
        def _():
            lax.fori_loop(0, 8, hots, 0)
            tick(0, 0)

        @pl.when(i == NB + 2)
        def _():
            tick(0, 1)

        return 0

    lax.fori_loop(0, NB + 4, step, 0)

    def rc(k, src, dst, to):
        return rcopy(src, dst, r_send.at[k], r_recv.at[k], to)

    def rgot(k, dst):
        rc(k, dst, dst, sib).wait_recv()

    def own_sum(b):
        v = segs[meta_ref[LAST, b]]
        return jnp.where(meta_ref[HAS, b] > 0, v, jnp.zeros_like(v))

    rcs = []

    def rstart(k, src, dst, to):
        cp = rc(k, src, dst, to)
        cp.start()
        rcs.append(cp)

    order = (1, 3, 2, 0)
    for d in order:
        theirs = lax.rem(s + d, 4)

        def give(n, _):
            xs[theirs * 8 + n] = own_sum(blk(1 - c, n // 2, theirs) + lax.rem(n, 2))
            return 0

        lax.fori_loop(0, 8, give, 0)
        piece = pl.ds(theirs * 8, 8)
        rstart(d, xs.at[piece], xr.at[piece], sib)
        if d == 1:
            tick(1, 0)

    def chip_sum(si, fi, h):
        return own_sum(blk(c, si, fi) + h).astype(F32) + xr[lax.rem(fi, 4) * 8 + lax.rem(si, 4) * 2 + h].astype(F32)

    for d in order:
        fi = lax.rem(f + d, 4)
        rgot(d, xr.at[pl.ds(fi * 8, 8)])
        for e in (2, 1, 3):
            for h in range(2):
                r1s[d, e, h] = chip_sum(s + e, fi, h).astype(BF16)
            rstart(4 + 4 * d + e, r1s.at[d, e], r1r.at[d, e], speer[e])
    tick(1, 1)
    tick(0, 3)
    cgrad_ref[...] = jnp.zeros_like(cgrad_ref)

    def ctx_dot(n, _):
        cgrad_ref[...] += jnp.dot(chot_a[n], call_a[n], preferred_element_type=F32)
        return 0

    def plane_sum(d, h):
        total = chip_sum(s, f + d, h)
        for e in turns:
            total += r1r[d, e, h].astype(F32)
        return total

    for d in order:
        for e in turns:
            rgot(4 + 4 * d + e, r1r.at[d, e])
        for h in range(2):
            if d:
                r2s[d, h] = plane_sum(d, h).astype(BF16)
            else:
                igrad_ref[pl.ds(h * SIDE, SIDE), :] = plane_sum(d, h)
        if d:
            rstart(20 + d, r2s.at[d], r2r.at[d], fpeer[d])
        if d == 1:
            tick(1, 2)
            lax.fori_loop(0, 32, ctx_dot, 0)
    tick(1, 3)
    for n in range(8):
        rows = call_b[pl.ds(4 * n, 4)].reshape(SIDE, WIDTH)
        cgrad_ref[...] += jnp.dot(chot_b[n], rows, preferred_element_type=F32)
    for d in turns:
        rgot(20 + d, r2r.at[d])
        igrad_ref[...] += r2r[d].reshape(2 * SIDE, WIDTH).astype(F32)

    for cp in started + rcs:
        cp.wait_send()
    for g in range(3):
        for k in (1, 2, 3, 5, 6, 7, 8):
            ccopies(g, k, False).wait_send()
    for ph in range(4):
        def drain(j, _):
            for cp in zcopies(ph, j):
                cp.wait_send()
            return 0

        lax.fori_loop(0, NB, drain, 0)


def hand_over(a_ref, b_ref, c_ref, a_out, b_out, c_out, sem):
    copies = [
        pltpu.make_async_copy(src, dst, sem.at[k])
        for k, (src, dst) in enumerate(((a_ref, a_out), (b_ref, b_out), (c_ref, c_out)))
    ]
    for cp in copies:
        cp.start()
    for cp in copies:
        cp.wait()


def local(
    user_factor,
    item_factor,
    context_factor,
    tile_user,
    tile_item,
    tile_context,
    tile_count,
    tile_mask,
    item_slot,
):
    n = tile_user.shape[0]
    nblocks = item_slot.shape[0]
    nctx = context_factor.shape[0]
    ids = jnp.arange(n, dtype=jnp.int32)
    hot_id = (tile_item[:, None] == jnp.arange(nblocks)[None, :]).astype(jnp.int32)
    slots = jnp.sum(hot_id * item_slot[None, :], axis=1)

    def place_of(block):
        owner, half = block // 2, block % 2
        core, xi, yi = owner % 2, owner // 8, (owner // 2) % 4
        fi = jnp.where(core == 0, xi, yi)
        si = jnp.where(core == 0, yi, xi)
        return ((core * 4 + si) * 4 + fi) * 2 + half

    place = place_of(slots)
    key = place * n + ids
    rank = jnp.sum((key[None, :] < key[:, None]).astype(jnp.int32), axis=1)
    pick = (rank[None, :] == ids[:, None]).astype(jnp.int32)
    live = (ids < tile_count[0]).astype(jnp.int32)
    vals = jnp.stack([place, tile_user, ids, live, tile_context])
    ordered = jnp.sum(pick[None] * vals[:, None, :], axis=2)
    place_s, ctx_s = ordered[PLACE], ordered[CTXT]
    before = jnp.concatenate([jnp.full((1,), -1, jnp.int32), place_s[:-1]])
    keep = (place_s == before).astype(jnp.int32)
    last = jnp.maximum(jnp.sum((place[None, :] <= ids[:, None]).astype(jnp.int32), axis=1) - 1, 0)
    has = jnp.any(place[None, :] == ids[:, None], axis=1).astype(jnp.int32)
    meta = jnp.concatenate([ordered, jnp.stack([keep, last, has])])
    rows = jnp.stack([ctx_s, jnp.tile(ctx_s[ROWS_A:], n // ROWS_B)])
    ids16 = jnp.pad(rows, ((0, 14), (0, 0))).astype(BF16)
    smem = pl.BlockSpec(memory_space=pltpu.SMEM)
    vmem = pl.BlockSpec(memory_space=pltpu.VMEM)
    tile2 = (SIDE, SIDE)
    wide = (SIDE, WIDTH)
    ugrad, igrad, cgrad = pl.pallas_call(
        kernel,
        out_shape=(
            jax.ShapeDtypeStruct((1024, WIDTH), F32),
            jax.ShapeDtypeStruct((2 * SIDE, WIDTH), F32),
            jax.ShapeDtypeStruct((nctx, WIDTH), F32),
        ),
        in_specs=[smem] + [vmem] * 4 + [pl.BlockSpec(memory_space=pl.ANY)],
        out_specs=(vmem,) * 3,
        scratch_shapes=[
            pltpu.VMEM((64,) + wide, BF16),
            pltpu.VMEM((n,) + tile2, jnp.int32),
            pltpu.VMEM((nctx, WIDTH), F32),
            pltpu.VMEM((4, 4, PER) + tile2, F32),
            pltpu.VMEM((NB, PER) + tile2, BF16),
            pltpu.VMEM((NB, 2, 2) + tile2, BF16),
            pltpu.VMEM((NB, 2, PER) + tile2, BF16),
            pltpu.VMEM((NB, 2, PER) + tile2, BF16),
            pltpu.VMEM((NB, 4, PER) + tile2, BF16),
            pltpu.VMEM(wide, F32),
            pltpu.VMEM((n,) + wide, BF16),
            pltpu.VMEM((1024, PER * SIDE), BF16),
            pltpu.VMEM((PER * SIDE, WIDTH), BF16),
            pltpu.VMEM(wide, F32),
            pltpu.VMEM((32,) + wide, BF16),
            pltpu.VMEM((32, 32, WIDTH), BF16),
            pltpu.VMEM((32, 16, SIDE), BF16),
            pltpu.VMEM((32, nctx, SIDE), BF16),
            pltpu.VMEM((8, nctx, SIDE), BF16),
            pltpu.VMEM((32,) + wide, BF16),
            pltpu.VMEM((32,) + wide, BF16),
            pltpu.VMEM((4, 4, 2) + wide, BF16),
            pltpu.VMEM((4, 4, 2) + wide, BF16),
            pltpu.VMEM((4, 2) + wide, BF16),
            pltpu.VMEM((4, 2) + wide, BF16),
            pltpu.SemaphoreType.DMA,
            pltpu.SemaphoreType.DMA((24,)),
            pltpu.SemaphoreType.DMA((24,)),
            pltpu.SemaphoreType.DMA((4, NB, 2)),
            pltpu.SemaphoreType.DMA((4, NB, 2)),
            pltpu.SemaphoreType.DMA((3, 9)),
            pltpu.SemaphoreType.DMA((3, 9)),
            pltpu.SemaphoreType.DMA((24,)),
            pltpu.SemaphoreType.DMA((24,)),
        ],
        compiler_params=pltpu.CompilerParams(
            collective_id=0, has_side_effects=True, vmem_limit_bytes=62 * 1024 * 1024
        ),
        cost_estimate=pl.CostEstimate(flops=10_000_000_000, bytes_accessed=20_000_000, transcendentals=0),
    )(
        meta,
        user_factor.reshape(-1, SIDE, WIDTH),
        item_factor.reshape(-1, SIDE, WIDTH),
        context_factor,
        ids16,
        tile_mask,
    )
    anywhere = pl.BlockSpec(memory_space=pl.ANY)
    return pl.pallas_call(
        hand_over,
        out_shape=tuple(jax.ShapeDtypeStruct(a.shape, a.dtype) for a in (ugrad, igrad, cgrad)),
        in_specs=[anywhere] * 3,
        out_specs=(anywhere,) * 3,
        scratch_shapes=[pltpu.SemaphoreType.DMA((3,))],
    )(ugrad, igrad, cgrad)


def solution(mesh):
    return jax.shard_map(
        local,
        mesh=mesh,
        in_specs=(
            P("tiles", "rank"),
            P("tiles", "rank"),
            P(None, "rank"),
            P("tiles"),
            P("tiles"),
            P("tiles"),
            P("tiles"),
            P("tiles", None, None),
            P(),
        ),
        out_specs=(P("tiles", "rank"), P("tiles", "rank"), P(None, "rank")),
        check_vma=False,
    )
```

```python
import functools

import jax
import jax.numpy as jnp
from jax import lax
from jax.experimental import pallas as pl
from jax.experimental.pallas import tpu as pltpu
from jax.sharding import PartitionSpec as P

MESH = pl.DeviceIdType.MESH
BF16 = jnp.bfloat16
F32 = jnp.float32
NB = 8
PER = 4
SIDE = 128
WIDTH = 256
ROWS_B = 32
ROWS_A = SIDE - ROWS_B
PLACE, USER, PERM, LIVE, CTXT, KEEP, LAST, HAS = range(8)


def kernel(
    meta_ref,
    users_ref,
    shard_ref,
    context_ref,
    ids_ref,
    mask_hbm,
    ugrad_ref,
    igrad_ref,
    cgrad_ref,
    items,
    mask,
    ctx32,
    part,
    send1,
    recv1,
    send2,
    recv2,
    resid,
    run,
    segs,
    ahot,
    icb,
    cterm,
    call_a,
    call_b,
    idall,
    chot_a,
    chot_b,
    xs,
    xr,
    r1s,
    r1r,
    r2s,
    r2r,
    mask_sem,
    ag_send,
    ag_recv,
    z_send,
    z_recv,
    c_send,
    c_recv,
    r_send,
    r_recv,
):
    z = lax.axis_index("rank")
    t = lax.axis_index("tiles")
    c = lax.rem(t, 2)
    y = lax.rem(t // 2, 4)
    x = t // 8
    f = x * (1 - c) + y * c
    s = y * (1 - c) + x * c

    def dev(fi, si):
        fi, si = lax.rem(fi + 4, 4), lax.rem(si + 4, 4)
        xi = fi * (1 - c) + si * c
        yi = si * (1 - c) + fi * c
        return {"rank": z, "tiles": (xi * 4 + yi) * 2 + c}

    def devz(d):
        return {"rank": lax.rem(z + d + 4, 4), "tiles": t}

    sib = {"rank": z, "tiles": t + 1 - 2 * c}
    turns = (1, 3, 2)
    fpeer = {d: dev(f + d, s) for d in turns}
    speer = {d: dev(f, s + d) for d in turns}
    partners = tuple(fpeer.values()) + tuple(speer.values()) + (devz(1), devz(-1), sib)
    mask_copy = pltpu.make_async_copy(mask_hbm, mask, mask_sem)
    mask_copy.start()
    barrier = pltpu.get_barrier_semaphore()
    for p in partners:
        pl.semaphore_signal(barrier, inc=1, device_id=p, device_id_type=MESH)
    pl.semaphore_wait(barrier, len(partners))

    def rcopy(src, dst, ss, rs, to):
        return pltpu.make_async_remote_copy(
            src_ref=src, dst_ref=dst, send_sem=ss, recv_sem=rs, device_id=to, device_id_type=MESH
        )

    started = []

    def blk(ci, si, fi):
        return ((ci * 4 + lax.rem(si + 4, 4)) * 4 + lax.rem(fi + 4, 4)) * 2

    def ag(k, start, size, to, src=None):
        view = items.at[pl.ds(start, size)]
        cp = rcopy(view if src is None else src, view, ag_send.at[k], ag_recv.at[k], to)
        cp.start()
        started.append(cp)

    def got(k, start, size):
        view = items.at[pl.ds(start, size)]
        rcopy(view, view, ag_send.at[k], ag_recv.at[k], sib).wait_recv()

    mine = blk(c, s, f)
    for d in turns:
        ag(d, mine, 2, fpeer[d], shard_ref)
    for d in turns:
        ag(4 + d, mine, 2, speer[d], shard_ref)
    items[pl.ds(mine, 2)] = shard_ref[...]
    ctx32[...] = context_ref[...].astype(F32)
    ugrad_ref[...] = jnp.zeros_like(ugrad_ref)
    run[...] = jnp.zeros_like(run)
    call_a[...] = jnp.zeros_like(call_a)
    for d in turns:
        e = 4 - d
        got(d, blk(c, s, f + e), 2)
        for dd in turns:
            ag(4 + 4 * e + dd, blk(c, s, f + e), 2, speer[dd])
    ag(20, blk(c, s, 0 * f), 8, sib)
    for d in turns:
        for e in (0, 3, 1, 2):
            got(4 + 4 * e + d, blk(c, s - d, f + e), 2)
        ag(20 + d, blk(c, s - d, 0 * f), 8, sib)
    for d in (0, 1, 3, 2):
        got(20 + d, blk(1 - c, f - d, 0 * f), 8)
    mask_copy.wait()

    right, left = devz(1), devz(-1)

    def zcopies(ph, j):
        o = z
        if ph == 0:
            return (
                rcopy(send1.at[j, pl.ds(0, 2)], recv1.at[j, 0], z_send.at[ph, j, 0], z_recv.at[ph, j, 0], right),
                rcopy(send1.at[j, pl.ds(2, 2)], recv1.at[j, 1], z_send.at[ph, j, 1], z_recv.at[ph, j, 1], left),
            )
        if ph == 1:
            return (
                rcopy(send2.at[j, 0], recv2.at[j, 0], z_send.at[ph, j, 0], z_recv.at[ph, j, 0], right),
                rcopy(send2.at[j, 1], recv2.at[j, 1], z_send.at[ph, j, 1], z_recv.at[ph, j, 1], left),
            )
        if ph == 2:
            return (
                rcopy(resid.at[j, o], resid.at[j, o], z_send.at[ph, j, 0], z_recv.at[ph, j, 0], right),
                rcopy(resid.at[j, o], resid.at[j, o], z_send.at[ph, j, 1], z_recv.at[ph, j, 1], left),
            )
        lo, hi = lax.rem(z + 3, 4), lax.rem(z + 1, 4)
        a = resid.at[j, lo, pl.ds(0, 2)]
        b = resid.at[j, hi, pl.ds(2, 2)]
        return (
            rcopy(a, a, z_send.at[ph, j, 0], z_recv.at[ph, j, 0], right),
            rcopy(b, b, z_send.at[ph, j, 1], z_recv.at[ph, j, 1], left),
        )

    def zwait(ph, j):
        lo, hi, far = lax.rem(z + 3, 4), lax.rem(z + 1, 4), lax.rem(z + 2, 4)
        if ph == 0:
            views = (recv1.at[j, 0], recv1.at[j, 1])
        elif ph == 1:
            views = (recv2.at[j, 0], recv2.at[j, 1])
        elif ph == 2:
            views = (resid.at[j, lo], resid.at[j, hi])
        else:
            views = (resid.at[j, far, pl.ds(0, 2)], resid.at[j, far, pl.ds(2, 2)])
        for d in range(2):
            rcopy(views[d], views[d], z_send.at[ph, j, d], z_recv.at[ph, j, d], right).wait_recv()

    def item_context(p):
        it = items[meta_ref[PLACE, p]].astype(F32)
        return (it * ctx32[pl.ds(meta_ref[CTXT, p], 1), :]).astype(BF16)

    def predict(j):
        slot = lax.rem(j, 4)

        def tile(n, _):
            o, k = n // PER, lax.rem(n, PER)
            p = j * 16 + n
            pr = lax.dot_general(
                users_ref[meta_ref[USER, p]], item_context(p), (((1,), (1,)), ((), ())), preferred_element_type=F32
            )
            part[slot, o, k] = pr
            return 0

        lax.fori_loop(0, 16, tile, 0)
        send1[j] = part[slot, lax.rem(z + 2, 4)].astype(BF16)
        for cp in zcopies(0, j):
            cp.start()

    def combine(j):
        slot = lax.rem(j, 4)
        hi, lo = lax.rem(z + 1, 4), lax.rem(z + 3, 4)
        zwait(0, j)
        send2[j, 0, pl.ds(0, 2)] = (part[slot, hi, pl.ds(0, 2)] + recv1[j, 0].astype(F32)).astype(BF16)
        send2[j, 0, pl.ds(2, 2)] = part[slot, hi, pl.ds(2, 2)].astype(BF16)
        send2[j, 1, pl.ds(0, 2)] = part[slot, lo, pl.ds(0, 2)].astype(BF16)
        send2[j, 1, pl.ds(2, 2)] = (part[slot, lo, pl.ds(2, 2)] + recv1[j, 1].astype(F32)).astype(BF16)
        for cp in zcopies(1, j):
            cp.start()

    def weigh(j):
        slot = lax.rem(j, 4)
        zwait(1, j)
        for k in range(PER):
            p = j * 16 + z * PER + k
            pr = part[slot, z, k] + recv2[j, 0, k].astype(F32) + recv2[j, 1, k].astype(F32)
            m = mask[meta_ref[PERM, p]].astype(F32)
            resid[j, z, k] = (meta_ref[LIVE, p].astype(F32) * (1.0 + 4.0 * m) * (pr - m) * (1.0 / 128.0)).astype(BF16)
        for cp in zcopies(2, j):
            cp.start()

    def forward(j):
        zwait(2, j)
        for cp in zcopies(3, j):
            cp.start()

    def gradients(j):
        zwait(3, j)

        def group(o, _):
            for k in range(PER):
                p = j * 16 + o * PER + k
                r = resid[j, o, k]
                u = meta_ref[USER, p]
                for b in range(8):
                    ahot[pl.ds(b * SIDE, SIDE), pl.ds(k * SIDE, SIDE)] = jnp.where(u == b, r, jnp.zeros_like(r))
                it = items[meta_ref[PLACE, p]].astype(F32)
                cr = ctx32[pl.ds(meta_ref[CTXT, p], 1), :]
                icb[pl.ds(k * SIDE, SIDE), :] = (it * cr).astype(BF16)
                q = lax.dot_general(r, users_ref[u], (((0,), (0,)), ((), ())), preferred_element_type=F32)
                cterm[pl.ds(p, 1), :] = jnp.sum(it * q, axis=0, keepdims=True)
                total = run[...] * meta_ref[KEEP, p].astype(F32) + q * cr
                run[...] = total
                segs[p] = total.astype(BF16)
            ugrad_ref[...] += jnp.dot(ahot[...], icb[...], preferred_element_type=F32)
            return 0

        lax.fori_loop(0, 4, group, 0)

    def ccopies(g, k, arriving):
        pos = lambda si, fi: (c * 4 + lax.rem(si + 4, 4)) * 4 + lax.rem(fi + 4, 4)
        if k < 4:
            at, count, to = (pos(s, f - k) if arriving else pos(s, f)), 1, fpeer[k]
        elif k < 8:
            at, count, to = (pos(s - (k - 4), 0 * f) if arriving else pos(s, 0 * f)), 4, speer[k - 4]
        else:
            at, count, to = ((1 - c) * 16 if arriving else c * 16), 16, sib
        if g == 0:
            a = call_a.at[pl.ds(at, count), pl.ds(0, ROWS_A)]
        else:
            a = (call_b if g == 1 else idall).at[pl.ds(at, count)]
        return rcopy(a, a, c_send.at[g, k], c_recv.at[g, k], to)

    def tick(g, n):
        own = (c * 4 + s) * 4 + f
        if n == 0:
            if g == 0:
                call_a[own, pl.ds(0, ROWS_A)] = cterm[pl.ds(0, ROWS_A), :].astype(BF16)
            elif g == 1:
                call_b[own] = cterm[pl.ds(ROWS_A, ROWS_B), :].astype(BF16)
            else:
                row = lax.broadcasted_iota(jnp.int32, (16, SIDE), 0)
                lane = lax.broadcasted_iota(jnp.int32, (16, SIDE), 1)
                hidden = (row == 1) & (lane // ROWS_B != f)
                idall[own] = jnp.where(hidden, 0.0, ids_ref[...].astype(F32)).astype(BF16)
        else:
            for d in turns if n < 3 else (0,):
                ccopies(g, 4 * (n - 1) + d, True).wait_recv()
        if n < 3:
            for d in turns if n < 2 else (0,):
                ccopies(g, 4 * n + d, False).start()

    def hot(ids):
        rows = lax.broadcasted_iota(jnp.int32, (WIDTH, SIDE), 0).astype(F32)
        return jnp.where(rows == ids, 1.0, 0.0).astype(BF16)

    def hots(n, _):
        rest = jnp.zeros((1, SIDE), F32)
        for k in range(4):
            both = idall[n * 4 + k].astype(F32)
            chot_a[n * 4 + k] = hot(both[0:1, :])
            rest += both[1:2, :]
        chot_b[n] = hot(rest)
        return 0

    def step(i, _):
        for n in range(4):

            @pl.when(i == 2 + n)
            def _():
                tick(2, n)

        @pl.when(i == NB + 3)
        def _():
            tick(0, 2)

        @pl.when(i < NB)
        def _():
            predict(i)

        @pl.when((i >= 1) & (i < NB + 1))
        def _():
            combine(i - 1)

        @pl.when((i >= 2) & (i < NB + 2))
        def _():
            weigh(i - 2)

        @pl.when((i >= 3) & (i < NB + 3))
        def _():
            forward(i - 3)

        @pl.when(i >= 4)
        def _():
            gradients(i - 4)

        @pl.when(i == NB + 1)
        def _():
            lax.fori_loop(0, 8, hots, 0)
            tick(0, 0)

        @pl.when(i == NB + 2)
        def _():
            tick(0, 1)

        return 0

    lax.fori_loop(0, NB + 4, step, 0)

    def rc(k, src, dst, to):
        return rcopy(src, dst, r_send.at[k], r_recv.at[k], to)

    def rgot(k, dst):
        rc(k, dst, dst, sib).wait_recv()

    def own_sum(b):
        v = segs[meta_ref[LAST, b]]
        return jnp.where(meta_ref[HAS, b] > 0, v, jnp.zeros_like(v))

    rcs = []

    def rstart(k, src, dst, to):
        cp = rc(k, src, dst, to)
        cp.start()
        rcs.append(cp)

    order = (1, 3, 2, 0)
    for d in order:
        theirs = lax.rem(s + d, 4)

        def give(n, _):
            xs[theirs * 8 + n] = own_sum(blk(1 - c, n // 2, theirs) + lax.rem(n, 2))
            return 0

        lax.fori_loop(0, 8, give, 0)
        piece = pl.ds(theirs * 8, 8)
        rstart(d, xs.at[piece], xr.at[piece], sib)
        if d == 1:
            tick(1, 0)

    def chip_sum(si, fi, h):
        return own_sum(blk(c, si, fi) + h).astype(F32) + xr[lax.rem(fi, 4) * 8 + lax.rem(si, 4) * 2 + h].astype(F32)

    for d in order:
        fi = lax.rem(f + d, 4)
        rgot(d, xr.at[pl.ds(fi * 8, 8)])
        for e in (2, 1, 3):
            for h in range(2):
                r1s[d, e, h] = chip_sum(s + e, fi, h).astype(BF16)
            rstart(4 + 4 * d + e, r1s.at[d, e], r1r.at[d, e], speer[e])
    tick(1, 1)
    tick(0, 3)
    cgrad_ref[...] = jnp.zeros_like(cgrad_ref)

    def ctx_dot(n, _):
        cgrad_ref[...] += jnp.dot(chot_a[n], call_a[n], preferred_element_type=F32)
        return 0

    def plane_sum(d, h):
        total = chip_sum(s, f + d, h)
        for e in turns:
            total += r1r[d, e, h].astype(F32)
        return total

    for d in order:
        for e in turns:
            rgot(4 + 4 * d + e, r1r.at[d, e])
        for h in range(2):
            if d:
                r2s[d, h] = plane_sum(d, h).astype(BF16)
            else:
                igrad_ref[pl.ds(h * SIDE, SIDE), :] = plane_sum(d, h)
        if d:
            rstart(20 + d, r2s.at[d], r2r.at[d], fpeer[d])
        if d == 1:
            tick(1, 2)
            lax.fori_loop(0, 32, ctx_dot, 0)
    tick(1, 3)
    for n in range(8):
        rows = call_b[pl.ds(4 * n, 4)].reshape(SIDE, WIDTH)
        cgrad_ref[...] += jnp.dot(chot_b[n], rows, preferred_element_type=F32)
    for d in turns:
        rgot(20 + d, r2r.at[d])
        igrad_ref[...] += r2r[d].reshape(2 * SIDE, WIDTH).astype(F32)

    for cp in started + rcs:
        cp.wait_send()
    for g in range(3):
        for k in (1, 2, 3, 5, 6, 7, 8):
            ccopies(g, k, False).wait_send()
    for ph in range(4):
        def drain(j, _):
            for cp in zcopies(ph, j):
                cp.wait_send()
            return 0

        lax.fori_loop(0, NB, drain, 0)


def hand_over(a_ref, b_ref, c_ref, a_out, b_out, c_out):
    a_out[...] = a_ref[...]
    b_out[...] = b_ref[...]
    c_out[...] = c_ref[...]


def local(
    user_factor,
    item_factor,
    context_factor,
    tile_user,
    tile_item,
    tile_context,
    tile_count,
    tile_mask,
    item_slot,
):
    n = tile_user.shape[0]
    nblocks = item_slot.shape[0]
    nctx = context_factor.shape[0]
    ids = jnp.arange(n, dtype=jnp.int32)
    hot_id = (tile_item[:, None] == jnp.arange(nblocks)[None, :]).astype(jnp.int32)
    slots = jnp.sum(hot_id * item_slot[None, :], axis=1)

    def place_of(block):
        owner, half = block // 2, block % 2
        core, xi, yi = owner % 2, owner // 8, (owner // 2) % 4
        fi = jnp.where(core == 0, xi, yi)
        si = jnp.where(core == 0, yi, xi)
        return ((core * 4 + si) * 4 + fi) * 2 + half

    place = place_of(slots)
    key = place * n + ids
    rank = jnp.sum((key[None, :] < key[:, None]).astype(jnp.int32), axis=1)
    pick = (rank[None, :] == ids[:, None]).astype(jnp.int32)
    live = (ids < tile_count[0]).astype(jnp.int32)
    vals = jnp.stack([place, tile_user, ids, live, tile_context])
    ordered = jnp.sum(pick[None] * vals[:, None, :], axis=2)
    place_s, ctx_s = ordered[PLACE], ordered[CTXT]
    before = jnp.concatenate([jnp.full((1,), -1, jnp.int32), place_s[:-1]])
    keep = (place_s == before).astype(jnp.int32)
    last = jnp.maximum(jnp.sum((place[None, :] <= ids[:, None]).astype(jnp.int32), axis=1) - 1, 0)
    has = jnp.any(place[None, :] == ids[:, None], axis=1).astype(jnp.int32)
    meta = jnp.concatenate([ordered, jnp.stack([keep, last, has])])
    rows = jnp.stack([ctx_s, jnp.tile(ctx_s[ROWS_A:], n // ROWS_B)])
    ids16 = jnp.pad(rows, ((0, 14), (0, 0))).astype(BF16)
    smem = pl.BlockSpec(memory_space=pltpu.SMEM)
    vmem = pl.BlockSpec(memory_space=pltpu.VMEM)
    tile2 = (SIDE, SIDE)
    wide = (SIDE, WIDTH)
    ugrad, igrad, cgrad = pl.pallas_call(
        kernel,
        out_shape=(
            jax.ShapeDtypeStruct((1024, WIDTH), F32),
            jax.ShapeDtypeStruct((2 * SIDE, WIDTH), F32),
            jax.ShapeDtypeStruct((nctx, WIDTH), F32),
        ),
        in_specs=[smem] + [vmem] * 4 + [pl.BlockSpec(memory_space=pl.ANY)],
        out_specs=(vmem,) * 3,
        scratch_shapes=[
            pltpu.VMEM((64,) + wide, BF16),
            pltpu.VMEM((n,) + tile2, jnp.int32),
            pltpu.VMEM((nctx, WIDTH), F32),
            pltpu.VMEM((4, 4, PER) + tile2, F32),
            pltpu.VMEM((NB, PER) + tile2, BF16),
            pltpu.VMEM((NB, 2, 2) + tile2, BF16),
            pltpu.VMEM((NB, 2, PER) + tile2, BF16),
            pltpu.VMEM((NB, 2, PER) + tile2, BF16),
            pltpu.VMEM((NB, 4, PER) + tile2, BF16),
            pltpu.VMEM(wide, F32),
            pltpu.VMEM((n,) + wide, BF16),
            pltpu.VMEM((1024, PER * SIDE), BF16),
            pltpu.VMEM((PER * SIDE, WIDTH), BF16),
            pltpu.VMEM(wide, F32),
            pltpu.VMEM((32,) + wide, BF16),
            pltpu.VMEM((32, 32, WIDTH), BF16),
            pltpu.VMEM((32, 16, SIDE), BF16),
            pltpu.VMEM((32, nctx, SIDE), BF16),
            pltpu.VMEM((8, nctx, SIDE), BF16),
            pltpu.VMEM((32,) + wide, BF16),
            pltpu.VMEM((32,) + wide, BF16),
            pltpu.VMEM((4, 4, 2) + wide, BF16),
            pltpu.VMEM((4, 4, 2) + wide, BF16),
            pltpu.VMEM((4, 2) + wide, BF16),
            pltpu.VMEM((4, 2) + wide, BF16),
            pltpu.SemaphoreType.DMA,
            pltpu.SemaphoreType.DMA((24,)),
            pltpu.SemaphoreType.DMA((24,)),
            pltpu.SemaphoreType.DMA((4, NB, 2)),
            pltpu.SemaphoreType.DMA((4, NB, 2)),
            pltpu.SemaphoreType.DMA((3, 9)),
            pltpu.SemaphoreType.DMA((3, 9)),
            pltpu.SemaphoreType.DMA((24,)),
            pltpu.SemaphoreType.DMA((24,)),
        ],
        compiler_params=pltpu.CompilerParams(
            collective_id=0, has_side_effects=True, vmem_limit_bytes=62 * 1024 * 1024
        ),
        cost_estimate=pl.CostEstimate(flops=10_000_000_000, bytes_accessed=20_000_000, transcendentals=0),
    )(
        meta,
        user_factor.reshape(-1, SIDE, WIDTH),
        item_factor.reshape(-1, SIDE, WIDTH),
        context_factor,
        ids16,
        tile_mask,
    )
    return pl.pallas_call(
        hand_over,
        out_shape=tuple(jax.ShapeDtypeStruct(a.shape, a.dtype) for a in (ugrad, igrad, cgrad)),
        in_specs=[vmem] * 3,
        out_specs=(vmem,) * 3,
    )(ugrad, igrad, cgrad)


def solution(mesh):
    return jax.shard_map(
        local,
        mesh=mesh,
        in_specs=(
            P("tiles", "rank"),
            P("tiles", "rank"),
            P(None, "rank"),
            P("tiles"),
            P("tiles"),
            P("tiles"),
            P("tiles"),
            P("tiles", None, None),
            P(),
        ),
        out_specs=(P("tiles", "rank"), P("tiles", "rank"), P(None, "rank")),
        check_vma=False,
    )
```

```python
import functools

import jax
import jax.numpy as jnp
from jax import lax
from jax.experimental import pallas as pl
from jax.experimental.pallas import tpu as pltpu
from jax.sharding import PartitionSpec as P

MESH = pl.DeviceIdType.MESH
BF16 = jnp.bfloat16
F32 = jnp.float32
NB = 8
PER = 4
SIDE = 128
WIDTH = 256
ROWS_B = 32
ROWS_A = SIDE - ROWS_B
PLACE, USER, PERM, LIVE, CTXT, KEEP, LAST, HAS = range(8)


def kernel(
    meta_ref,
    users_ref,
    shard_ref,
    context_ref,
    ids_ref,
    mask_hbm,
    ugrad_ref,
    igrad_ref,
    cgrad_ref,
    items,
    mask,
    ctx32,
    part,
    send1,
    recv1,
    send2,
    recv2,
    resid,
    run,
    segs,
    ahot,
    icb,
    cterm,
    call_a,
    call_b,
    idall,
    chot_a,
    chot_b,
    xs,
    xr,
    r1s,
    r1r,
    r2s,
    r2r,
    mask_sem,
    ag_send,
    ag_recv,
    z_send,
    z_recv,
    c_send,
    c_recv,
    r_send,
    r_recv,
):
    z = lax.axis_index("rank")
    t = lax.axis_index("tiles")
    c = lax.rem(t, 2)
    y = lax.rem(t // 2, 4)
    x = t // 8
    f = x * (1 - c) + y * c
    s = y * (1 - c) + x * c

    def dev(fi, si):
        fi, si = lax.rem(fi + 4, 4), lax.rem(si + 4, 4)
        xi = fi * (1 - c) + si * c
        yi = si * (1 - c) + fi * c
        return {"rank": z, "tiles": (xi * 4 + yi) * 2 + c}

    def devz(d):
        return {"rank": lax.rem(z + d + 4, 4), "tiles": t}

    sib = {"rank": z, "tiles": t + 1 - 2 * c}
    turns = (1, 3, 2)
    fpeer = {d: dev(f + d, s) for d in turns}
    speer = {d: dev(f, s + d) for d in turns}
    partners = tuple(fpeer.values()) + tuple(speer.values()) + (devz(1), devz(-1), sib)
    mask_copy = pltpu.make_async_copy(mask_hbm, mask, mask_sem)
    mask_copy.start()
    barrier = pltpu.get_barrier_semaphore()
    for p in partners:
        pl.semaphore_signal(barrier, inc=1, device_id=p, device_id_type=MESH)
    pl.semaphore_wait(barrier, len(partners))

    def rcopy(src, dst, ss, rs, to):
        return pltpu.make_async_remote_copy(
            src_ref=src, dst_ref=dst, send_sem=ss, recv_sem=rs, device_id=to, device_id_type=MESH
        )

    started = []

    def blk(ci, si, fi):
        return ((ci * 4 + lax.rem(si + 4, 4)) * 4 + lax.rem(fi + 4, 4)) * 2

    def ag(k, start, size, to, src=None):
        view = items.at[pl.ds(start, size)]
        cp = rcopy(view if src is None else src, view, ag_send.at[k], ag_recv.at[k], to)
        cp.start()
        started.append(cp)

    def got(k, start, size):
        view = items.at[pl.ds(start, size)]
        rcopy(view, view, ag_send.at[k], ag_recv.at[k], sib).wait_recv()

    mine = blk(c, s, f)
    for d in turns:
        ag(d, mine, 2, fpeer[d], shard_ref)
    for d in turns:
        ag(4 + d, mine, 2, speer[d], shard_ref)
    items[pl.ds(mine, 2)] = shard_ref[...]
    ctx32[...] = context_ref[...].astype(F32)
    ugrad_ref[...] = jnp.zeros_like(ugrad_ref)
    run[...] = jnp.zeros_like(run)
    call_a[...] = jnp.zeros_like(call_a)
    for d in turns:
        e = 4 - d
        got(d, blk(c, s, f + e), 2)
        for dd in turns:
            ag(4 + 4 * e + dd, blk(c, s, f + e), 2, speer[dd])
    ag(20, blk(c, s, 0 * f), 8, sib)
    for d in turns:
        for e in (0, 3, 1, 2):
            got(4 + 4 * e + d, blk(c, s - d, f + e), 2)
        ag(20 + d, blk(c, s - d, 0 * f), 8, sib)
    for d in (0, 1, 3, 2):
        got(20 + d, blk(1 - c, f - d, 0 * f), 8)
    mask_copy.wait()

    right, left = devz(1), devz(-1)

    def zcopies(ph, j):
        o = z
        if ph == 0:
            return (
                rcopy(send1.at[j, pl.ds(0, 2)], recv1.at[j, 0], z_send.at[ph, j, 0], z_recv.at[ph, j, 0], right),
                rcopy(send1.at[j, pl.ds(2, 2)], recv1.at[j, 1], z_send.at[ph, j, 1], z_recv.at[ph, j, 1], left),
            )
        if ph == 1:
            return (
                rcopy(send2.at[j, 0], recv2.at[j, 0], z_send.at[ph, j, 0], z_recv.at[ph, j, 0], right),
                rcopy(send2.at[j, 1], recv2.at[j, 1], z_send.at[ph, j, 1], z_recv.at[ph, j, 1], left),
            )
        if ph == 2:
            return (
                rcopy(resid.at[j, o], resid.at[j, o], z_send.at[ph, j, 0], z_recv.at[ph, j, 0], right),
                rcopy(resid.at[j, o], resid.at[j, o], z_send.at[ph, j, 1], z_recv.at[ph, j, 1], left),
            )
        lo, hi = lax.rem(z + 3, 4), lax.rem(z + 1, 4)
        a = resid.at[j, lo, pl.ds(0, 2)]
        b = resid.at[j, hi, pl.ds(2, 2)]
        return (
            rcopy(a, a, z_send.at[ph, j, 0], z_recv.at[ph, j, 0], right),
            rcopy(b, b, z_send.at[ph, j, 1], z_recv.at[ph, j, 1], left),
        )

    def zwait(ph, j):
        lo, hi, far = lax.rem(z + 3, 4), lax.rem(z + 1, 4), lax.rem(z + 2, 4)
        if ph == 0:
            views = (recv1.at[j, 0], recv1.at[j, 1])
        elif ph == 1:
            views = (recv2.at[j, 0], recv2.at[j, 1])
        elif ph == 2:
            views = (resid.at[j, lo], resid.at[j, hi])
        else:
            views = (resid.at[j, far, pl.ds(0, 2)], resid.at[j, far, pl.ds(2, 2)])
        for d in range(2):
            rcopy(views[d], views[d], z_send.at[ph, j, d], z_recv.at[ph, j, d], right).wait_recv()

    def item_context(p):
        it = items[meta_ref[PLACE, p]].astype(F32)
        return (it * ctx32[pl.ds(meta_ref[CTXT, p], 1), :]).astype(BF16)

    def predict(j):
        slot = lax.rem(j, 4)

        def tile(n, _):
            o, k = n // PER, lax.rem(n, PER)
            p = j * 16 + n
            pr = lax.dot_general(
                users_ref[meta_ref[USER, p]], item_context(p), (((1,), (1,)), ((), ())), preferred_element_type=F32
            )
            part[slot, o, k] = pr
            return 0

        lax.fori_loop(0, 16, tile, 0)
        send1[j] = part[slot, lax.rem(z + 2, 4)].astype(BF16)
        for cp in zcopies(0, j):
            cp.start()

    def combine(j):
        slot = lax.rem(j, 4)
        hi, lo = lax.rem(z + 1, 4), lax.rem(z + 3, 4)
        zwait(0, j)
        send2[j, 0, pl.ds(0, 2)] = (part[slot, hi, pl.ds(0, 2)] + recv1[j, 0].astype(F32)).astype(BF16)
        send2[j, 0, pl.ds(2, 2)] = part[slot, hi, pl.ds(2, 2)].astype(BF16)
        send2[j, 1, pl.ds(0, 2)] = part[slot, lo, pl.ds(0, 2)].astype(BF16)
        send2[j, 1, pl.ds(2, 2)] = (part[slot, lo, pl.ds(2, 2)] + recv1[j, 1].astype(F32)).astype(BF16)
        for cp in zcopies(1, j):
            cp.start()

    def weigh(j):
        slot = lax.rem(j, 4)
        zwait(1, j)
        for k in range(PER):
            p = j * 16 + z * PER + k
            pr = part[slot, z, k] + recv2[j, 0, k].astype(F32) + recv2[j, 1, k].astype(F32)
            m = mask[meta_ref[PERM, p]].astype(F32)
            resid[j, z, k] = (meta_ref[LIVE, p].astype(F32) * (1.0 + 4.0 * m) * (pr - m) * (1.0 / 128.0)).astype(BF16)
        for cp in zcopies(2, j):
            cp.start()

    def forward(j):
        zwait(2, j)
        for cp in zcopies(3, j):
            cp.start()

    def gradients(j):
        zwait(3, j)

        def group(o, _):
            for k in range(PER):
                p = j * 16 + o * PER + k
                r = resid[j, o, k]
                u = meta_ref[USER, p]
                for b in range(8):
                    ahot[pl.ds(b * SIDE, SIDE), pl.ds(k * SIDE, SIDE)] = jnp.where(u == b, r, jnp.zeros_like(r))
                it = items[meta_ref[PLACE, p]].astype(F32)
                cr = ctx32[pl.ds(meta_ref[CTXT, p], 1), :]
                icb[pl.ds(k * SIDE, SIDE), :] = (it * cr).astype(BF16)
                q = lax.dot_general(r, users_ref[u], (((0,), (0,)), ((), ())), preferred_element_type=F32)
                cterm[pl.ds(p, 1), :] = jnp.sum(it * q, axis=0, keepdims=True)
                total = run[...] * meta_ref[KEEP, p].astype(F32) + q * cr
                run[...] = total
                segs[p] = total.astype(BF16)
            ugrad_ref[...] += jnp.dot(ahot[...], icb[...], preferred_element_type=F32)
            return 0

        lax.fori_loop(0, 4, group, 0)

    def ccopies(g, k, arriving):
        pos = lambda si, fi: (c * 4 + lax.rem(si + 4, 4)) * 4 + lax.rem(fi + 4, 4)
        if k < 4:
            at, count, to = (pos(s, f - k) if arriving else pos(s, f)), 1, fpeer[k]
        elif k < 8:
            at, count, to = (pos(s - (k - 4), 0 * f) if arriving else pos(s, 0 * f)), 4, speer[k - 4]
        else:
            at, count, to = ((1 - c) * 16 if arriving else c * 16), 16, sib
        if g == 0:
            a = call_a.at[pl.ds(at, count), pl.ds(0, ROWS_A)]
        else:
            a = (call_b if g == 1 else idall).at[pl.ds(at, count)]
        return rcopy(a, a, c_send.at[g, k], c_recv.at[g, k], to)

    def tick(g, n):
        own = (c * 4 + s) * 4 + f
        if n == 0:
            if g == 0:
                call_a[own, pl.ds(0, ROWS_A)] = cterm[pl.ds(0, ROWS_A), :].astype(BF16)
            elif g == 1:
                call_b[own] = cterm[pl.ds(ROWS_A, ROWS_B), :].astype(BF16)
            else:
                row = lax.broadcasted_iota(jnp.int32, (16, SIDE), 0)
                lane = lax.broadcasted_iota(jnp.int32, (16, SIDE), 1)
                hidden = (row == 1) & (lane // ROWS_B != f)
                idall[own] = jnp.where(hidden, 0.0, ids_ref[...].astype(F32)).astype(BF16)
        else:
            for d in turns if n < 3 else (0,):
                ccopies(g, 4 * (n - 1) + d, True).wait_recv()
        if n < 3:
            for d in turns if n < 2 else (0,):
                ccopies(g, 4 * n + d, False).start()

    def hot(ids):
        rows = lax.broadcasted_iota(jnp.int32, (WIDTH, SIDE), 0).astype(F32)
        return jnp.where(rows == ids, 1.0, 0.0).astype(BF16)

    def hots(n, _):
        rest = jnp.zeros((1, SIDE), F32)
        for k in range(4):
            both = idall[n * 4 + k].astype(F32)
            chot_a[n * 4 + k] = hot(both[0:1, :])
            rest += both[1:2, :]
        chot_b[n] = hot(rest)
        return 0

    def step(i, _):
        for n in range(4):

            @pl.when(i == 2 + n)
            def _():
                tick(2, n)

        @pl.when(i == NB + 3)
        def _():
            tick(0, 2)

        @pl.when(i < NB)
        def _():
            predict(i)

        @pl.when((i >= 1) & (i < NB + 1))
        def _():
            combine(i - 1)

        @pl.when((i >= 2) & (i < NB + 2))
        def _():
            weigh(i - 2)

        @pl.when((i >= 3) & (i < NB + 3))
        def _():
            forward(i - 3)

        @pl.when(i >= 4)
        def _():
            gradients(i - 4)

        @pl.when(i == NB + 1)
        def _():
            lax.fori_loop(0, 8, hots, 0)
            tick(0, 0)

        @pl.when(i == NB + 2)
        def _():
            tick(0, 1)

        return 0

    lax.fori_loop(0, NB + 4, step, 0)

    def rc(k, src, dst, to):
        return rcopy(src, dst, r_send.at[k], r_recv.at[k], to)

    def rgot(k, dst):
        rc(k, dst, dst, sib).wait_recv()

    def own_sum(b):
        v = segs[meta_ref[LAST, b]]
        return jnp.where(meta_ref[HAS, b] > 0, v, jnp.zeros_like(v))

    rcs = []

    def rstart(k, src, dst, to):
        cp = rc(k, src, dst, to)
        cp.start()
        rcs.append(cp)

    tick(1, 0)
    order = (1, 3, 2, 0)
    for d in order:
        theirs = lax.rem(s + d, 4)

        def give(n, _):
            xs[theirs * 8 + n] = own_sum(blk(1 - c, n // 2, theirs) + lax.rem(n, 2))
            return 0

        lax.fori_loop(0, 8, give, 0)
        piece = pl.ds(theirs * 8, 8)
        rstart(d, xs.at[piece], xr.at[piece], sib)

    def chip_sum(si, fi, h):
        return own_sum(blk(c, si, fi) + h).astype(F32) + xr[lax.rem(fi, 4) * 8 + lax.rem(si, 4) * 2 + h].astype(F32)

    for d in order:
        fi = lax.rem(f + d, 4)
        rgot(d, xr.at[pl.ds(fi * 8, 8)])
        for e in (2, 1, 3):
            for h in range(2):
                r1s[d, e, h] = chip_sum(s + e, fi, h).astype(BF16)
            rstart(4 + 4 * d + e, r1s.at[d, e], r1r.at[d, e], speer[e])
        if d == 1:
            tick(1, 1)
    tick(0, 3)
    cgrad_ref[...] = jnp.zeros_like(cgrad_ref)

    def ctx_dot(n, _):
        cgrad_ref[...] += jnp.dot(chot_a[n], call_a[n], preferred_element_type=F32)
        return 0

    lax.fori_loop(0, 32, ctx_dot, 0)

    def plane_sum(d, h):
        total = chip_sum(s, f + d, h)
        for e in turns:
            total += r1r[d, e, h].astype(F32)
        return total

    for d in order:
        for e in turns:
            rgot(4 + 4 * d + e, r1r.at[d, e])
        for h in range(2):
            if d:
                r2s[d, h] = plane_sum(d, h).astype(BF16)
            else:
                igrad_ref[pl.ds(h * SIDE, SIDE), :] = plane_sum(d, h)
        if d:
            rstart(20 + d, r2s.at[d], r2r.at[d], fpeer[d])
        if d == 2:
            tick(1, 2)
    tick(1, 3)
    for n in range(8):
        rows = call_b[pl.ds(4 * n, 4)].reshape(SIDE, WIDTH)
        cgrad_ref[...] += jnp.dot(chot_b[n], rows, preferred_element_type=F32)
    for d in turns:
        rgot(20 + d, r2r.at[d])
        igrad_ref[...] += r2r[d].reshape(2 * SIDE, WIDTH).astype(F32)

    for cp in started + rcs:
        cp.wait_send()
    for g in range(3):
        for k in (1, 2, 3, 5, 6, 7, 8):
            ccopies(g, k, False).wait_send()
    for ph in range(4):
        def drain(j, _):
            for cp in zcopies(ph, j):
                cp.wait_send()
            return 0

        lax.fori_loop(0, NB, drain, 0)


def hand_over(a_ref, b_ref, c_ref, a_out, b_out, c_out):
    a_out[...] = a_ref[...]
    b_out[...] = b_ref[...]
    c_out[...] = c_ref[...]


def local(
    user_factor,
    item_factor,
    context_factor,
    tile_user,
    tile_item,
    tile_context,
    tile_count,
    tile_mask,
    item_slot,
):
    n = tile_user.shape[0]
    nblocks = item_slot.shape[0]
    nctx = context_factor.shape[0]
    ids = jnp.arange(n, dtype=jnp.int32)
    hot_id = (tile_item[:, None] == jnp.arange(nblocks)[None, :]).astype(jnp.int32)
    slots = jnp.sum(hot_id * item_slot[None, :], axis=1)

    def place_of(block):
        owner, half = block // 2, block % 2
        core, xi, yi = owner % 2, owner // 8, (owner // 2) % 4
        fi = jnp.where(core == 0, xi, yi)
        si = jnp.where(core == 0, yi, xi)
        return ((core * 4 + si) * 4 + fi) * 2 + half

    place = place_of(slots)
    key = place * n + ids
    rank = jnp.sum((key[None, :] < key[:, None]).astype(jnp.int32), axis=1)
    pick = (rank[None, :] == ids[:, None]).astype(jnp.int32)
    live = (ids < tile_count[0]).astype(jnp.int32)
    vals = jnp.stack([place, tile_user, ids, live, tile_context])
    ordered = jnp.sum(pick[None] * vals[:, None, :], axis=2)
    place_s, ctx_s = ordered[PLACE], ordered[CTXT]
    before = jnp.concatenate([jnp.full((1,), -1, jnp.int32), place_s[:-1]])
    keep = (place_s == before).astype(jnp.int32)
    last = jnp.maximum(jnp.sum((place[None, :] <= ids[:, None]).astype(jnp.int32), axis=1) - 1, 0)
    has = jnp.any(place[None, :] == ids[:, None], axis=1).astype(jnp.int32)
    meta = jnp.concatenate([ordered, jnp.stack([keep, last, has])])
    rows = jnp.stack([ctx_s, jnp.tile(ctx_s[ROWS_A:], n // ROWS_B)])
    ids16 = jnp.pad(rows, ((0, 14), (0, 0))).astype(BF16)
    smem = pl.BlockSpec(memory_space=pltpu.SMEM)
    vmem = pl.BlockSpec(memory_space=pltpu.VMEM)
    tile2 = (SIDE, SIDE)
    wide = (SIDE, WIDTH)
    ugrad, igrad, cgrad = pl.pallas_call(
        kernel,
        out_shape=(
            jax.ShapeDtypeStruct((1024, WIDTH), F32),
            jax.ShapeDtypeStruct((2 * SIDE, WIDTH), F32),
            jax.ShapeDtypeStruct((nctx, WIDTH), F32),
        ),
        in_specs=[smem] + [vmem] * 4 + [pl.BlockSpec(memory_space=pl.ANY)],
        out_specs=(vmem,) * 3,
        scratch_shapes=[
            pltpu.VMEM((64,) + wide, BF16),
            pltpu.VMEM((n,) + tile2, jnp.int32),
            pltpu.VMEM((nctx, WIDTH), F32),
            pltpu.VMEM((4, 4, PER) + tile2, F32),
            pltpu.VMEM((NB, PER) + tile2, BF16),
            pltpu.VMEM((NB, 2, 2) + tile2, BF16),
            pltpu.VMEM((NB, 2, PER) + tile2, BF16),
            pltpu.VMEM((NB, 2, PER) + tile2, BF16),
            pltpu.VMEM((NB, 4, PER) + tile2, BF16),
            pltpu.VMEM(wide, F32),
            pltpu.VMEM((n,) + wide, BF16),
            pltpu.VMEM((1024, PER * SIDE), BF16),
            pltpu.VMEM((PER * SIDE, WIDTH), BF16),
            pltpu.VMEM(wide, F32),
            pltpu.VMEM((32,) + wide, BF16),
            pltpu.VMEM((32, 32, WIDTH), BF16),
            pltpu.VMEM((32, 16, SIDE), BF16),
            pltpu.VMEM((32, nctx, SIDE), BF16),
            pltpu.VMEM((8, nctx, SIDE), BF16),
            pltpu.VMEM((32,) + wide, BF16),
            pltpu.VMEM((32,) + wide, BF16),
            pltpu.VMEM((4, 4, 2) + wide, BF16),
            pltpu.VMEM((4, 4, 2) + wide, BF16),
            pltpu.VMEM((4, 2) + wide, BF16),
            pltpu.VMEM((4, 2) + wide, BF16),
            pltpu.SemaphoreType.DMA,
            pltpu.SemaphoreType.DMA((24,)),
            pltpu.SemaphoreType.DMA((24,)),
            pltpu.SemaphoreType.DMA((4, NB, 2)),
            pltpu.SemaphoreType.DMA((4, NB, 2)),
            pltpu.SemaphoreType.DMA((3, 9)),
            pltpu.SemaphoreType.DMA((3, 9)),
            pltpu.SemaphoreType.DMA((24,)),
            pltpu.SemaphoreType.DMA((24,)),
        ],
        compiler_params=pltpu.CompilerParams(
            collective_id=0, has_side_effects=True, vmem_limit_bytes=62 * 1024 * 1024
        ),
        cost_estimate=pl.CostEstimate(flops=10_000_000_000, bytes_accessed=20_000_000, transcendentals=0),
    )(
        meta,
        user_factor.reshape(-1, SIDE, WIDTH),
        item_factor.reshape(-1, SIDE, WIDTH),
        context_factor,
        ids16,
        tile_mask,
    )
    return pl.pallas_call(
        hand_over,
        out_shape=tuple(jax.ShapeDtypeStruct(a.shape, a.dtype) for a in (ugrad, igrad, cgrad)),
        in_specs=[vmem] * 3,
        out_specs=(vmem,) * 3,
    )(ugrad, igrad, cgrad)


def solution(mesh):
    return jax.shard_map(
        local,
        mesh=mesh,
        in_specs=(
            P("tiles", "rank"),
            P("tiles", "rank"),
            P(None, "rank"),
            P("tiles"),
            P("tiles"),
            P("tiles"),
            P("tiles"),
            P("tiles", None, None),
            P(),
        ),
        out_specs=(P("tiles", "rank"), P("tiles", "rank"), P(None, "rank")),
        check_vma=False,
    )
```

```python
import functools

import jax
import jax.numpy as jnp
from jax import lax
from jax.experimental import pallas as pl
from jax.experimental.pallas import tpu as pltpu
from jax.sharding import PartitionSpec as P

MESH = pl.DeviceIdType.MESH
BF16 = jnp.bfloat16
F32 = jnp.float32
NB = 8
PER = 4
SIDE = 128
WIDTH = 256
ROWS_B = 32
ROWS_A = SIDE - ROWS_B
PLACE, USER, PERM, LIVE, CTXT, KEEP, LAST, HAS = range(8)


def kernel(
    meta_ref,
    users_in,
    shard_in,
    context_in,
    ids_in,
    mask_in,
    ugrad_out,
    igrad_out,
    cgrad_out,
    users_ref,
    context_ref,
    ids_ref,
    ugrad_ref,
    igrad_ref,
    cgrad_ref,
    items,
    mask,
    ctx32,
    part,
    send1,
    recv1,
    send2,
    recv2,
    resid,
    run,
    segs,
    ahot,
    icb,
    cterm,
    call_a,
    call_b,
    idall,
    chot_a,
    chot_b,
    xs,
    xr,
    r1s,
    r1r,
    r2s,
    r2r,
    in_sem,
    out_sem,
    ag_send,
    ag_recv,
    z_send,
    z_recv,
    c_send,
    c_recv,
    r_send,
    r_recv,
):
    z = lax.axis_index("rank")
    t = lax.axis_index("tiles")
    c = lax.rem(t, 2)
    y = lax.rem(t // 2, 4)
    x = t // 8
    f = x * (1 - c) + y * c
    s = y * (1 - c) + x * c

    def dev(fi, si):
        fi, si = lax.rem(fi + 4, 4), lax.rem(si + 4, 4)
        xi = fi * (1 - c) + si * c
        yi = si * (1 - c) + fi * c
        return {"rank": z, "tiles": (xi * 4 + yi) * 2 + c}

    def devz(d):
        return {"rank": lax.rem(z + d + 4, 4), "tiles": t}

    sib = {"rank": z, "tiles": t + 1 - 2 * c}
    turns = (1, 3, 2)
    fpeer = {d: dev(f + d, s) for d in turns}
    speer = {d: dev(f, s + d) for d in turns}
    partners = tuple(fpeer.values()) + tuple(speer.values()) + (devz(1), devz(-1), sib)
    mine = ((c * 4 + s) * 4 + f) * 2
    fetch = [
        pltpu.make_async_copy(src, dst, in_sem.at[k])
        for k, (src, dst) in enumerate(
            (
                (shard_in, items.at[pl.ds(mine, 2)]),
                (context_in, context_ref),
                (ids_in, ids_ref),
                (users_in, users_ref),
                (mask_in, mask),
            )
        )
    ]
    for cp in fetch:
        cp.start()
    barrier = pltpu.get_barrier_semaphore()
    for p in partners:
        pl.semaphore_signal(barrier, inc=1, device_id=p, device_id_type=MESH)
    pl.semaphore_wait(barrier, len(partners))

    def rcopy(src, dst, ss, rs, to):
        return pltpu.make_async_remote_copy(
            src_ref=src, dst_ref=dst, send_sem=ss, recv_sem=rs, device_id=to, device_id_type=MESH
        )

    started = []

    def blk(ci, si, fi):
        return ((ci * 4 + lax.rem(si + 4, 4)) * 4 + lax.rem(fi + 4, 4)) * 2

    def ag(k, start, size, to):
        view = items.at[pl.ds(start, size)]
        cp = rcopy(view, view, ag_send.at[k], ag_recv.at[k], to)
        cp.start()
        started.append(cp)

    def got(k, start, size):
        view = items.at[pl.ds(start, size)]
        rcopy(view, view, ag_send.at[k], ag_recv.at[k], sib).wait_recv()

    fetch[0].wait()
    for d in turns:
        ag(d, mine, 2, fpeer[d])
    for d in turns:
        ag(4 + d, mine, 2, speer[d])
    fetch[1].wait()
    ctx32[...] = context_ref[...].astype(F32)
    ugrad_ref[...] = jnp.zeros_like(ugrad_ref)
    run[...] = jnp.zeros_like(run)
    call_a[...] = jnp.zeros_like(call_a)
    for d in turns:
        e = 4 - d
        got(d, blk(c, s, f + e), 2)
        for dd in turns:
            ag(4 + 4 * e + dd, blk(c, s, f + e), 2, speer[dd])
    ag(20, blk(c, s, 0 * f), 8, sib)
    last = tuple(zip((0, 3, 1, 2), (22, 24, 25, 26)))
    for d in turns:
        for e, k in last:
            got(4 + 4 * e + d, blk(c, s - d, f + e), 2)
            if d == 2:
                ag(k, blk(c, s - d, f + e), 2, sib)
        if d != 2:
            ag(20 + d, blk(c, s - d, 0 * f), 8, sib)
    for d in (0, 1, 3):
        got(20 + d, blk(1 - c, f - d, 0 * f), 8)
    for e, k in last:
        got(k, blk(1 - c, f - 2, s + e), 2)
    for cp in fetch[2:]:
        cp.wait()

    right, left = devz(1), devz(-1)

    def zcopies(ph, j):
        o = z
        if ph == 0:
            return (
                rcopy(send1.at[j, pl.ds(0, 2)], recv1.at[j, 0], z_send.at[ph, j, 0], z_recv.at[ph, j, 0], right),
                rcopy(send1.at[j, pl.ds(2, 2)], recv1.at[j, 1], z_send.at[ph, j, 1], z_recv.at[ph, j, 1], left),
            )
        if ph == 1:
            return (
                rcopy(send2.at[j, 0], recv2.at[j, 0], z_send.at[ph, j, 0], z_recv.at[ph, j, 0], right),
                rcopy(send2.at[j, 1], recv2.at[j, 1], z_send.at[ph, j, 1], z_recv.at[ph, j, 1], left),
            )
        if ph == 2:
            return (
                rcopy(resid.at[j, o], resid.at[j, o], z_send.at[ph, j, 0], z_recv.at[ph, j, 0], right),
                rcopy(resid.at[j, o], resid.at[j, o], z_send.at[ph, j, 1], z_recv.at[ph, j, 1], left),
            )
        lo, hi = lax.rem(z + 3, 4), lax.rem(z + 1, 4)
        a = resid.at[j, lo, pl.ds(0, 2)]
        b = resid.at[j, hi, pl.ds(2, 2)]
        return (
            rcopy(a, a, z_send.at[ph, j, 0], z_recv.at[ph, j, 0], right),
            rcopy(b, b, z_send.at[ph, j, 1], z_recv.at[ph, j, 1], left),
        )

    def zwait(ph, j):
        lo, hi, far = lax.rem(z + 3, 4), lax.rem(z + 1, 4), lax.rem(z + 2, 4)
        if ph == 0:
            views = (recv1.at[j, 0], recv1.at[j, 1])
        elif ph == 1:
            views = (recv2.at[j, 0], recv2.at[j, 1])
        elif ph == 2:
            views = (resid.at[j, lo], resid.at[j, hi])
        else:
            views = (resid.at[j, far, pl.ds(0, 2)], resid.at[j, far, pl.ds(2, 2)])
        for d in range(2):
            rcopy(views[d], views[d], z_send.at[ph, j, d], z_recv.at[ph, j, d], right).wait_recv()

    def item_context(p):
        it = items[meta_ref[PLACE, p]].astype(F32)
        return (it * ctx32[pl.ds(meta_ref[CTXT, p], 1), :]).astype(BF16)

    def predict(j):
        slot = lax.rem(j, 4)

        far = lax.rem(z + 2, 4)

        def tile(n, _):
            o, k = lax.rem(far + n // PER, 4), lax.rem(n, PER)
            p = j * 16 + o * PER + k
            pr = lax.dot_general(
                users_ref[meta_ref[USER, p]], item_context(p), (((1,), (1,)), ((), ())), preferred_element_type=F32
            )
            part[slot, o, k] = pr
            return 0

        lax.fori_loop(0, PER, tile, 0)
        send1[j] = part[slot, far].astype(BF16)
        for cp in zcopies(0, j):
            cp.start()
        lax.fori_loop(PER, 16, tile, 0)

    def combine(j):
        slot = lax.rem(j, 4)
        hi, lo = lax.rem(z + 1, 4), lax.rem(z + 3, 4)
        zwait(0, j)
        send2[j, 0, pl.ds(0, 2)] = (part[slot, hi, pl.ds(0, 2)] + recv1[j, 0].astype(F32)).astype(BF16)
        send2[j, 0, pl.ds(2, 2)] = part[slot, hi, pl.ds(2, 2)].astype(BF16)
        send2[j, 1, pl.ds(0, 2)] = part[slot, lo, pl.ds(0, 2)].astype(BF16)
        send2[j, 1, pl.ds(2, 2)] = (part[slot, lo, pl.ds(2, 2)] + recv1[j, 1].astype(F32)).astype(BF16)
        for cp in zcopies(1, j):
            cp.start()

    def weigh(j):
        slot = lax.rem(j, 4)
        zwait(1, j)
        for k in range(PER):
            p = j * 16 + z * PER + k
            pr = part[slot, z, k] + recv2[j, 0, k].astype(F32) + recv2[j, 1, k].astype(F32)
            m = mask[meta_ref[PERM, p]].astype(F32)
            resid[j, z, k] = (meta_ref[LIVE, p].astype(F32) * (1.0 + 4.0 * m) * (pr - m) * (1.0 / 128.0)).astype(BF16)
        for cp in zcopies(2, j):
            cp.start()

    def forward(j):
        zwait(2, j)
        for cp in zcopies(3, j):
            cp.start()

    def user_part(j, o):
        for k in range(PER):
            p = j * 16 + o * PER + k
            r = resid[j, o, k]
            u = meta_ref[USER, p]
            for b in range(8):
                ahot[pl.ds(b * SIDE, SIDE), pl.ds(k * SIDE, SIDE)] = jnp.where(u == b, r, jnp.zeros_like(r))
            icb[pl.ds(k * SIDE, SIDE), :] = item_context(p)
        ugrad_ref[...] += jnp.dot(ahot[...], icb[...], preferred_element_type=F32)

    def item_part(j, o):
        for k in range(PER):
            p = j * 16 + o * PER + k
            it = items[meta_ref[PLACE, p]].astype(F32)
            cr = ctx32[pl.ds(meta_ref[CTXT, p], 1), :]
            q = lax.dot_general(
                resid[j, o, k], users_ref[meta_ref[USER, p]], (((0,), (0,)), ((), ())), preferred_element_type=F32
            )
            cterm[pl.ds(p, 1), :] = jnp.sum(it * q, axis=0, keepdims=True)
            total = run[...] * meta_ref[KEEP, p].astype(F32) + q * cr
            run[...] = total
            segs[p] = total.astype(BF16)

    def gradients(j):
        def near(n, _):
            user_part(j, lax.rem(z + 3 + n, 4))
            return 0

        def group(o, _):
            item_part(j, o)
            return 0

        lax.fori_loop(0, 3, near, 0)
        zwait(3, j)
        lax.fori_loop(0, 4, group, 0)
        user_part(j, lax.rem(z + 2, 4))

    def ccopies(g, k, arriving):
        pos = lambda si, fi: (c * 4 + lax.rem(si + 4, 4)) * 4 + lax.rem(fi + 4, 4)
        if k < 4:
            at, count, to = (pos(s, f - k) if arriving else pos(s, f)), 1, fpeer[k]
        elif k < 8:
            at, count, to = (pos(s - (k - 4), 0 * f) if arriving else pos(s, 0 * f)), 4, speer[k - 4]
        else:
            at, count, to = ((1 - c) * 16 if arriving else c * 16), 16, sib
        if g == 0:
            a = call_a.at[pl.ds(at, count), pl.ds(0, ROWS_A)]
        else:
            a = (call_b if g == 1 else idall).at[pl.ds(at, count)]
        return rcopy(a, a, c_send.at[g, k], c_recv.at[g, k], to)

    def tick(g, n):
        own = (c * 4 + s) * 4 + f
        if n == 0:
            if g == 0:
                call_a[own, pl.ds(0, ROWS_A)] = cterm[pl.ds(0, ROWS_A), :].astype(BF16)
            elif g == 1:
                call_b[own] = cterm[pl.ds(ROWS_A, ROWS_B), :].astype(BF16)
            else:
                row = lax.broadcasted_iota(jnp.int32, (16, SIDE), 0)
                lane = lax.broadcasted_iota(jnp.int32, (16, SIDE), 1)
                hidden = (row == 1) & (lane // ROWS_B != f)
                idall[own] = jnp.where(hidden, 0.0, ids_ref[...].astype(F32)).astype(BF16)
        else:
            for d in turns if n < 3 else (0,):
                ccopies(g, 4 * (n - 1) + d, True).wait_recv()
        if n < 3:
            for d in turns if n < 2 else (0,):
                ccopies(g, 4 * n + d, False).start()

    def hot(ids):
        rows = lax.broadcasted_iota(jnp.int32, (WIDTH, SIDE), 0).astype(F32)
        return jnp.where(rows == ids, 1.0, 0.0).astype(BF16)

    def hots(n, _):
        rest = jnp.zeros((1, SIDE), F32)
        for k in range(4):
            both = idall[n * 4 + k].astype(F32)
            chot_a[n * 4 + k] = hot(both[0:1, :])
            rest += both[1:2, :]
        chot_b[n] = hot(rest)
        return 0

    def step(i, _):
        for n in range(4):

            @pl.when(i == 2 + n)
            def _():
                tick(2, n)

        @pl.when(i == NB + 3)
        def _():
            tick(0, 2)

        @pl.when(i < NB)
        def _():
            predict(i)

        @pl.when((i >= 1) & (i < NB + 1))
        def _():
            combine(i - 1)

        @pl.when((i >= 2) & (i < NB + 2))
        def _():
            weigh(i - 2)

        @pl.when((i >= 3) & (i < NB + 3))
        def _():
            forward(i - 3)

        @pl.when(i >= 4)
        def _():
            gradients(i - 4)

        @pl.when(i == NB + 1)
        def _():
            lax.fori_loop(0, 8, hots, 0)
            tick(0, 0)

        @pl.when(i == NB + 2)
        def _():
            tick(0, 1)

        return 0

    lax.fori_loop(0, NB + 4, step, 0)

    def rc(k, src, dst, to):
        return rcopy(src, dst, r_send.at[k], r_recv.at[k], to)

    def rgot(k, dst):
        rc(k, dst, dst, sib).wait_recv()

    def own_sum(b):
        v = segs[meta_ref[LAST, b]]
        return jnp.where(meta_ref[HAS, b] > 0, v, jnp.zeros_like(v))

    rcs = []

    def rstart(k, src, dst, to):
        cp = rc(k, src, dst, to)
        cp.start()
        rcs.append(cp)

    tick(1, 0)
    results = [
        pltpu.make_async_copy(src, dst, out_sem.at[k])
        for k, (src, dst) in enumerate(((ugrad_ref, ugrad_out), (igrad_ref, igrad_out), (cgrad_ref, cgrad_out)))
    ]
    results[0].start()
    order = (1, 3, 2, 0)

    def give_piece(d):
        theirs = lax.rem(s + d, 4)

        def give(n, _):
            xs[theirs * 8 + n] = own_sum(blk(1 - c, n // 2, theirs) + lax.rem(n, 2))
            return 0

        lax.fori_loop(0, 8, give, 0)
        piece = pl.ds(theirs * 8, 8)
        rstart(d, xs.at[piece], xr.at[piece], sib)

    give_piece(1)
    give_piece(3)

    def chip_sum(si, fi, h):
        return own_sum(blk(c, si, fi) + h).astype(F32) + xr[lax.rem(fi, 4) * 8 + lax.rem(si, 4) * 2 + h].astype(F32)

    for d in order:
        fi = lax.rem(f + d, 4)
        rgot(d, xr.at[pl.ds(fi * 8, 8)])
        for e in (2, 1, 3):
            for h in range(2):
                r1s[d, e, h] = chip_sum(s + e, fi, h).astype(BF16)
            rstart(4 + 4 * d + e, r1s.at[d, e], r1r.at[d, e], speer[e])
        if d == 1:
            give_piece(2)
            tick(1, 1)
        if d == 3:
            give_piece(0)
    tick(0, 3)
    cgrad_ref[...] = jnp.zeros_like(cgrad_ref)

    def ctx_dot(n, _):
        cgrad_ref[...] += jnp.dot(chot_a[n], call_a[n], preferred_element_type=F32)
        return 0

    lax.fori_loop(0, 32, ctx_dot, 0)

    def plane_sum(d, h):
        total = chip_sum(s, f + d, h)
        for e in turns:
            total += r1r[d, e, h].astype(F32)
        return total

    for d in order:
        for e in turns:
            rgot(4 + 4 * d + e, r1r.at[d, e])
        for h in range(2):
            if d:
                r2s[d, h] = plane_sum(d, h).astype(BF16)
            else:
                igrad_ref[pl.ds(h * SIDE, SIDE), :] = plane_sum(d, h)
        if d:
            rstart(20 + d, r2s.at[d], r2r.at[d], fpeer[d])
        if d == 2:
            tick(1, 2)
    tick(1, 3)
    for n in range(8):
        rows = call_b[pl.ds(4 * n, 4)].reshape(SIDE, WIDTH)
        cgrad_ref[...] += jnp.dot(chot_b[n], rows, preferred_element_type=F32)
    for d in turns:
        rgot(20 + d, r2r.at[d])
        igrad_ref[...] += r2r[d].reshape(2 * SIDE, WIDTH).astype(F32)

    results[1].start()
    results[2].start()
    for cp in started + rcs:
        cp.wait_send()
    for g in range(3):
        for k in (1, 2, 3, 5, 6, 7, 8):
            ccopies(g, k, False).wait_send()
    for ph in range(4):
        def drain(j, _):
            for cp in zcopies(ph, j):
                cp.wait_send()
            return 0

        lax.fori_loop(0, NB, drain, 0)
    for cp in results:
        cp.wait()


def hand_over(*refs):
    srcs, dsts, bufs, sem = refs[:3], refs[3:6], refs[6:9], refs[9]
    reads = [pltpu.make_async_copy(a, b, sem.at[0, k]) for k, (a, b) in enumerate(zip(srcs, bufs))]
    writes = [pltpu.make_async_copy(a, b, sem.at[1, k]) for k, (a, b) in enumerate(zip(bufs, dsts))]
    for cp in reads:
        cp.start()
    for a, b in zip(reads, writes):
        a.wait()
        b.start()
    for cp in writes:
        cp.wait()


def local(
    user_factor,
    item_factor,
    context_factor,
    tile_user,
    tile_item,
    tile_context,
    tile_count,
    tile_mask,
    item_slot,
):
    n = tile_user.shape[0]
    nblocks = item_slot.shape[0]
    nctx = context_factor.shape[0]
    ids = jnp.arange(n, dtype=jnp.int32)
    hot_id = (tile_item[:, None] == jnp.arange(nblocks)[None, :]).astype(jnp.int32)
    slots = jnp.sum(hot_id * item_slot[None, :], axis=1)

    def place_of(block):
        owner, half = block // 2, block % 2
        core, xi, yi = owner % 2, owner // 8, (owner // 2) % 4
        fi = jnp.where(core == 0, xi, yi)
        si = jnp.where(core == 0, yi, xi)
        return ((core * 4 + si) * 4 + fi) * 2 + half

    place = place_of(slots)
    key = place * n + ids
    rank = jnp.sum((key[None, :] < key[:, None]).astype(jnp.int32), axis=1)
    pick = (rank[None, :] == ids[:, None]).astype(jnp.int32)
    live = (ids < tile_count[0]).astype(jnp.int32)
    vals = jnp.stack([place, tile_user, ids, live, tile_context])
    ordered = jnp.sum(pick[None] * vals[:, None, :], axis=2)
    place_s, ctx_s = ordered[PLACE], ordered[CTXT]
    before = jnp.concatenate([jnp.full((1,), -1, jnp.int32), place_s[:-1]])
    keep = (place_s == before).astype(jnp.int32)
    last = jnp.maximum(jnp.sum((place[None, :] <= ids[:, None]).astype(jnp.int32), axis=1) - 1, 0)
    has = jnp.any(place[None, :] == ids[:, None], axis=1).astype(jnp.int32)
    meta = jnp.concatenate([ordered, jnp.stack([keep, last, has])])
    rows = jnp.stack([ctx_s, jnp.tile(ctx_s[ROWS_A:], n // ROWS_B)])
    ids16 = jnp.pad(rows, ((0, 14), (0, 0))).astype(BF16)
    smem = pl.BlockSpec(memory_space=pltpu.SMEM)
    anywhere = pl.BlockSpec(memory_space=pl.ANY)
    tile2 = (SIDE, SIDE)
    wide = (SIDE, WIDTH)
    ugrad, igrad, cgrad = pl.pallas_call(
        kernel,
        out_shape=(
            jax.ShapeDtypeStruct((1024, WIDTH), F32),
            jax.ShapeDtypeStruct((2 * SIDE, WIDTH), F32),
            jax.ShapeDtypeStruct((nctx, WIDTH), F32),
        ),
        in_specs=[smem] + [anywhere] * 5,
        out_specs=(anywhere,) * 3,
        scratch_shapes=[
            pltpu.VMEM((8,) + wide, BF16),
            pltpu.VMEM((nctx, WIDTH), BF16),
            pltpu.VMEM((16, SIDE), BF16),
            pltpu.VMEM((1024, WIDTH), F32),
            pltpu.VMEM((2 * SIDE, WIDTH), F32),
            pltpu.VMEM((nctx, WIDTH), F32),
            pltpu.VMEM((64,) + wide, BF16),
            pltpu.VMEM((n,) + tile2, jnp.int32),
            pltpu.VMEM((nctx, WIDTH), F32),
            pltpu.VMEM((4, 4, PER) + tile2, F32),
            pltpu.VMEM((NB, PER) + tile2, BF16),
            pltpu.VMEM((NB, 2, 2) + tile2, BF16),
            pltpu.VMEM((NB, 2, PER) + tile2, BF16),
            pltpu.VMEM((NB, 2, PER) + tile2, BF16),
            pltpu.VMEM((NB, 4, PER) + tile2, BF16),
            pltpu.VMEM(wide, F32),
            pltpu.VMEM((n,) + wide, BF16),
            pltpu.VMEM((1024, PER * SIDE), BF16),
            pltpu.VMEM((PER * SIDE, WIDTH), BF16),
            pltpu.VMEM(wide, F32),
            pltpu.VMEM((32,) + wide, BF16),
            pltpu.VMEM((32, 32, WIDTH), BF16),
            pltpu.VMEM((32, 16, SIDE), BF16),
            pltpu.VMEM((32, nctx, SIDE), BF16),
            pltpu.VMEM((8, nctx, SIDE), BF16),
            pltpu.VMEM((32,) + wide, BF16),
            pltpu.VMEM((32,) + wide, BF16),
            pltpu.VMEM((4, 4, 2) + wide, BF16),
            pltpu.VMEM((4, 4, 2) + wide, BF16),
            pltpu.VMEM((4, 2) + wide, BF16),
            pltpu.VMEM((4, 2) + wide, BF16),
            pltpu.SemaphoreType.DMA((5,)),
            pltpu.SemaphoreType.DMA((3,)),
            pltpu.SemaphoreType.DMA((27,)),
            pltpu.SemaphoreType.DMA((27,)),
            pltpu.SemaphoreType.DMA((4, NB, 2)),
            pltpu.SemaphoreType.DMA((4, NB, 2)),
            pltpu.SemaphoreType.DMA((3, 9)),
            pltpu.SemaphoreType.DMA((3, 9)),
            pltpu.SemaphoreType.DMA((24,)),
            pltpu.SemaphoreType.DMA((24,)),
        ],
        compiler_params=pltpu.CompilerParams(
            collective_id=0, has_side_effects=True, vmem_limit_bytes=62 * 1024 * 1024
        ),
        cost_estimate=pl.CostEstimate(flops=10_000_000_000, bytes_accessed=20_000_000, transcendentals=0),
    )(
        meta,
        user_factor.reshape(-1, SIDE, WIDTH),
        item_factor.reshape(-1, SIDE, WIDTH),
        context_factor,
        ids16,
        tile_mask,
    )
    return pl.pallas_call(
        hand_over,
        out_shape=tuple(jax.ShapeDtypeStruct(a.shape, a.dtype) for a in (ugrad, igrad, cgrad)),
        in_specs=[anywhere] * 3,
        out_specs=(anywhere,) * 3,
        scratch_shapes=[pltpu.VMEM(a.shape, a.dtype) for a in (ugrad, igrad, cgrad)]
        + [pltpu.SemaphoreType.DMA((2, 3))],
    )(ugrad, igrad, cgrad)


def solution(mesh):
    return jax.shard_map(
        local,
        mesh=mesh,
        in_specs=(
            P("tiles", "rank"),
            P("tiles", "rank"),
            P(None, "rank"),
            P("tiles"),
            P("tiles"),
            P("tiles"),
            P("tiles"),
            P("tiles", None, None),
            P(),
        ),
        out_specs=(P("tiles", "rank"), P("tiles", "rank"), P(None, "rank")),
        check_vma=False,
    )
```

```python
import functools

import jax
import jax.numpy as jnp
from jax import lax
from jax.experimental import pallas as pl
from jax.experimental.pallas import tpu as pltpu
from jax.sharding import PartitionSpec as P

MESH = pl.DeviceIdType.MESH
BF16 = jnp.bfloat16
F32 = jnp.float32
NB = 8
PER = 4
SIDE = 128
WIDTH = 256
ROWS_B = 32
ROWS_A = SIDE - ROWS_B
PLACE, USER, PERM, LIVE, CTXT, KEEP, LAST, HAS = range(8)


def kernel(
    meta_ref,
    users_in,
    shard_in,
    context_in,
    ids_in,
    mask_in,
    ugrad_out,
    igrad_out,
    cgrad_out,
    users_ref,
    context_ref,
    ids_ref,
    ugrad_ref,
    igrad_ref,
    cgrad_ref,
    items,
    mask,
    ctx32,
    part,
    send1,
    recv1,
    send2,
    recv2,
    resid,
    run,
    segs,
    ahot,
    icb,
    cterm,
    call_a,
    call_b,
    idall,
    chot_a,
    chot_b,
    xs,
    xr,
    r1s,
    r1r,
    r2s,
    r2r,
    in_sem,
    out_sem,
    ag_send,
    ag_recv,
    z_send,
    z_recv,
    c_send,
    c_recv,
    r_send,
    r_recv,
):
    z = lax.axis_index("rank")
    t = lax.axis_index("tiles")
    c = lax.rem(t, 2)
    y = lax.rem(t // 2, 4)
    x = t // 8
    f = x * (1 - c) + y * c
    s = y * (1 - c) + x * c

    def dev(fi, si):
        fi, si = lax.rem(fi + 4, 4), lax.rem(si + 4, 4)
        xi = fi * (1 - c) + si * c
        yi = si * (1 - c) + fi * c
        return {"rank": z, "tiles": (xi * 4 + yi) * 2 + c}

    def devz(d):
        return {"rank": lax.rem(z + d + 4, 4), "tiles": t}

    sib = {"rank": z, "tiles": t + 1 - 2 * c}
    turns = (1, 3, 2)
    fpeer = {d: dev(f + d, s) for d in turns}
    speer = {d: dev(f, s + d) for d in turns}
    partners = tuple(fpeer.values()) + tuple(speer.values()) + (devz(1), devz(-1), sib)
    mine = ((c * 4 + s) * 4 + f) * 2
    fetch = [
        pltpu.make_async_copy(src, dst, in_sem.at[k])
        for k, (src, dst) in enumerate(
            (
                (shard_in, items.at[pl.ds(mine, 2)]),
                (context_in, context_ref),
                (ids_in, ids_ref),
                (users_in, users_ref),
                (mask_in, mask),
            )
        )
    ]
    for cp in fetch:
        cp.start()
    barrier = pltpu.get_barrier_semaphore()
    for p in partners:
        pl.semaphore_signal(barrier, inc=1, device_id=p, device_id_type=MESH)
    pl.semaphore_wait(barrier, len(partners))

    def rcopy(src, dst, ss, rs, to):
        return pltpu.make_async_remote_copy(
            src_ref=src, dst_ref=dst, send_sem=ss, recv_sem=rs, device_id=to, device_id_type=MESH
        )

    started = []

    def blk(ci, si, fi):
        return ((ci * 4 + lax.rem(si + 4, 4)) * 4 + lax.rem(fi + 4, 4)) * 2

    def ag(k, start, size, to):
        view = items.at[pl.ds(start, size)]
        cp = rcopy(view, view, ag_send.at[k], ag_recv.at[k], to)
        cp.start()
        started.append(cp)

    def got(k, start, size):
        view = items.at[pl.ds(start, size)]
        rcopy(view, view, ag_send.at[k], ag_recv.at[k], sib).wait_recv()

    fetch[0].wait()
    for d in turns:
        ag(d, mine, 2, fpeer[d])
    for d in turns:
        ag(4 + d, mine, 2, speer[d])
    fetch[1].wait()
    ctx32[...] = context_ref[...].astype(F32)
    ugrad_ref[...] = jnp.zeros_like(ugrad_ref)
    run[...] = jnp.zeros_like(run)
    call_a[...] = jnp.zeros_like(call_a)
    for d in turns:
        e = 4 - d
        got(d, blk(c, s, f + e), 2)
        for dd in turns:
            ag(4 + 4 * e + dd, blk(c, s, f + e), 2, speer[dd])
    ag(20, blk(c, s, 0 * f), 8, sib)
    last = tuple(zip((0, 3, 1, 2), (22, 24, 25, 26)))
    for d in turns:
        for e, k in last:
            got(4 + 4 * e + d, blk(c, s - d, f + e), 2)
            if d == 2:
                ag(k, blk(c, s - d, f + e), 2, sib)
        if d != 2:
            ag(20 + d, blk(c, s - d, 0 * f), 8, sib)
    for d in (0, 1, 3):
        got(20 + d, blk(1 - c, f - d, 0 * f), 8)
    for e, k in last:
        got(k, blk(1 - c, f - 2, s + e), 2)
    for cp in fetch[2:]:
        cp.wait()

    right, left = devz(1), devz(-1)

    def zcopies(ph, j):
        o = z
        if ph == 0:
            return (
                rcopy(send1.at[j, pl.ds(0, 2)], recv1.at[j, 0], z_send.at[ph, j, 0], z_recv.at[ph, j, 0], right),
                rcopy(send1.at[j, pl.ds(2, 2)], recv1.at[j, 1], z_send.at[ph, j, 1], z_recv.at[ph, j, 1], left),
            )
        if ph == 1:
            return (
                rcopy(send2.at[j, 0], recv2.at[j, 0], z_send.at[ph, j, 0], z_recv.at[ph, j, 0], right),
                rcopy(send2.at[j, 1], recv2.at[j, 1], z_send.at[ph, j, 1], z_recv.at[ph, j, 1], left),
            )
        if ph == 2:
            return (
                rcopy(resid.at[j, o], resid.at[j, o], z_send.at[ph, j, 0], z_recv.at[ph, j, 0], right),
                rcopy(resid.at[j, o], resid.at[j, o], z_send.at[ph, j, 1], z_recv.at[ph, j, 1], left),
            )
        lo, hi = lax.rem(z + 3, 4), lax.rem(z + 1, 4)
        a = resid.at[j, lo, pl.ds(0, 2)]
        b = resid.at[j, hi, pl.ds(2, 2)]
        return (
            rcopy(a, a, z_send.at[ph, j, 0], z_recv.at[ph, j, 0], right),
            rcopy(b, b, z_send.at[ph, j, 1], z_recv.at[ph, j, 1], left),
        )

    def zwait(ph, j):
        lo, hi, far = lax.rem(z + 3, 4), lax.rem(z + 1, 4), lax.rem(z + 2, 4)
        if ph == 0:
            views = (recv1.at[j, 0], recv1.at[j, 1])
        elif ph == 1:
            views = (recv2.at[j, 0], recv2.at[j, 1])
        elif ph == 2:
            views = (resid.at[j, lo], resid.at[j, hi])
        else:
            views = (resid.at[j, far, pl.ds(0, 2)], resid.at[j, far, pl.ds(2, 2)])
        for d in range(2):
            rcopy(views[d], views[d], z_send.at[ph, j, d], z_recv.at[ph, j, d], right).wait_recv()

    def item_context(p):
        it = items[meta_ref[PLACE, p]].astype(F32)
        return (it * ctx32[pl.ds(meta_ref[CTXT, p], 1), :]).astype(BF16)

    def predict(j):
        slot = lax.rem(j, 4)

        far = lax.rem(z + 2, 4)

        def tile(n, _):
            o, k = lax.rem(far + n // PER, 4), lax.rem(n, PER)
            p = j * 16 + o * PER + k
            pr = lax.dot_general(
                users_ref[meta_ref[USER, p]], item_context(p), (((1,), (1,)), ((), ())), preferred_element_type=F32
            )
            part[slot, o, k] = pr
            return 0

        lax.fori_loop(0, PER, tile, 0)
        send1[j] = part[slot, far].astype(BF16)
        for cp in zcopies(0, j):
            cp.start()
        lax.fori_loop(PER, 16, tile, 0)

    def combine(j):
        slot = lax.rem(j, 4)
        hi, lo = lax.rem(z + 1, 4), lax.rem(z + 3, 4)
        zwait(0, j)
        send2[j, 0, pl.ds(0, 2)] = (part[slot, hi, pl.ds(0, 2)] + recv1[j, 0].astype(F32)).astype(BF16)
        send2[j, 0, pl.ds(2, 2)] = part[slot, hi, pl.ds(2, 2)].astype(BF16)
        send2[j, 1, pl.ds(0, 2)] = part[slot, lo, pl.ds(0, 2)].astype(BF16)
        send2[j, 1, pl.ds(2, 2)] = (part[slot, lo, pl.ds(2, 2)] + recv1[j, 1].astype(F32)).astype(BF16)
        for cp in zcopies(1, j):
            cp.start()

    def weigh(j):
        slot = lax.rem(j, 4)
        zwait(1, j)
        for k in range(PER):
            p = j * 16 + z * PER + k
            pr = part[slot, z, k] + recv2[j, 0, k].astype(F32) + recv2[j, 1, k].astype(F32)
            m = mask[meta_ref[PERM, p]].astype(F32)
            resid[j, z, k] = (meta_ref[LIVE, p].astype(F32) * (1.0 + 4.0 * m) * (pr - m) * (1.0 / 128.0)).astype(BF16)
        for cp in zcopies(2, j):
            cp.start()

    def forward(j):
        zwait(2, j)
        for cp in zcopies(3, j):
            cp.start()

    def user_part(j, o):
        for k in range(PER):
            p = j * 16 + o * PER + k
            r = resid[j, o, k]
            u = meta_ref[USER, p]
            for b in range(8):
                ahot[pl.ds(b * SIDE, SIDE), pl.ds(k * SIDE, SIDE)] = jnp.where(u == b, r, jnp.zeros_like(r))
            icb[pl.ds(k * SIDE, SIDE), :] = item_context(p)
        ugrad_ref[...] += jnp.dot(ahot[...], icb[...], preferred_element_type=F32)

    def item_part(j, o):
        for k in range(PER):
            p = j * 16 + o * PER + k
            it = items[meta_ref[PLACE, p]].astype(F32)
            cr = ctx32[pl.ds(meta_ref[CTXT, p], 1), :]
            q = lax.dot_general(
                resid[j, o, k], users_ref[meta_ref[USER, p]], (((0,), (0,)), ((), ())), preferred_element_type=F32
            )
            cterm[pl.ds(p, 1), :] = jnp.sum(it * q, axis=0, keepdims=True)
            total = run[...] * meta_ref[KEEP, p].astype(F32) + q * cr
            run[...] = total
            segs[p] = total.astype(BF16)

    def gradients(j):
        def near(n, _):
            user_part(j, lax.rem(z + 3 + n, 4))
            return 0

        def group(o, _):
            item_part(j, o)
            return 0

        lax.fori_loop(0, 3, near, 0)
        zwait(3, j)
        lax.fori_loop(0, 4, group, 0)
        user_part(j, lax.rem(z + 2, 4))

    def ccopies(g, k, arriving):
        pos = lambda si, fi: (c * 4 + lax.rem(si + 4, 4)) * 4 + lax.rem(fi + 4, 4)
        if k < 4:
            at, count, to = (pos(s, f - k) if arriving else pos(s, f)), 1, fpeer[k]
        elif k < 8:
            at, count, to = (pos(s - (k - 4), 0 * f) if arriving else pos(s, 0 * f)), 4, speer[k - 4]
        else:
            at, count, to = ((1 - c) * 16 if arriving else c * 16), 16, sib
        if g == 0:
            a = call_a.at[pl.ds(at, count), pl.ds(0, ROWS_A)]
        else:
            a = (call_b if g == 1 else idall).at[pl.ds(at, count)]
        return rcopy(a, a, c_send.at[g, k], c_recv.at[g, k], to)

    def tick(g, n):
        own = (c * 4 + s) * 4 + f
        if n == 0:
            if g == 0:
                call_a[own, pl.ds(0, ROWS_A)] = cterm[pl.ds(0, ROWS_A), :].astype(BF16)
            elif g == 1:
                call_b[own] = cterm[pl.ds(ROWS_A, ROWS_B), :].astype(BF16)
            else:
                row = lax.broadcasted_iota(jnp.int32, (16, SIDE), 0)
                lane = lax.broadcasted_iota(jnp.int32, (16, SIDE), 1)
                hidden = (row == 1) & (lane // ROWS_B != f)
                idall[own] = jnp.where(hidden, 0.0, ids_ref[...].astype(F32)).astype(BF16)
        else:
            for d in turns if n < 3 else (0,):
                ccopies(g, 4 * (n - 1) + d, True).wait_recv()
        if n < 3:
            for d in turns if n < 2 else (0,):
                ccopies(g, 4 * n + d, False).start()

    def hot(ids):
        rows = lax.broadcasted_iota(jnp.int32, (WIDTH, SIDE), 0).astype(F32)
        return jnp.where(rows == ids, 1.0, 0.0).astype(BF16)

    def hots(n, _):
        rest = jnp.zeros((1, SIDE), F32)
        for k in range(4):
            both = idall[n * 4 + k].astype(F32)
            chot_a[n * 4 + k] = hot(both[0:1, :])
            rest += both[1:2, :]
        chot_b[n] = hot(rest)
        return 0

    def step(i, _):
        for n in range(4):

            @pl.when(i == 2 + n)
            def _():
                tick(2, n)

        @pl.when(i == NB + 3)
        def _():
            tick(0, 2)

        @pl.when(i < NB)
        def _():
            predict(i)

        @pl.when((i >= 1) & (i < NB + 1))
        def _():
            combine(i - 1)

        @pl.when((i >= 2) & (i < NB + 2))
        def _():
            weigh(i - 2)

        @pl.when((i >= 3) & (i < NB + 3))
        def _():
            forward(i - 3)

        @pl.when(i >= 4)
        def _():
            gradients(i - 4)

        @pl.when(i == NB + 1)
        def _():
            lax.fori_loop(0, 8, hots, 0)
            tick(0, 0)

        @pl.when(i == NB + 2)
        def _():
            tick(0, 1)

        return 0

    lax.fori_loop(0, NB + 4, step, 0)

    def rc(k, src, dst, to):
        return rcopy(src, dst, r_send.at[k], r_recv.at[k], to)

    def rgot(k, dst):
        rc(k, dst, dst, sib).wait_recv()

    def own_sum(b):
        v = segs[meta_ref[LAST, b]]
        return jnp.where(meta_ref[HAS, b] > 0, v, jnp.zeros_like(v))

    rcs = []

    def rstart(k, src, dst, to):
        cp = rc(k, src, dst, to)
        cp.start()
        rcs.append(cp)

    tick(1, 0)
    results = [
        pltpu.make_async_copy(src, dst, out_sem.at[k])
        for k, (src, dst) in enumerate(((ugrad_ref, ugrad_out), (igrad_ref, igrad_out), (cgrad_ref, cgrad_out)))
    ]
    results[0].start()
    order = (1, 3, 2, 0)

    def give_piece(d):
        theirs = lax.rem(s + d, 4)

        def give(n, _):
            xs[theirs * 8 + n] = own_sum(blk(1 - c, n // 2, theirs) + lax.rem(n, 2))
            return 0

        lax.fori_loop(0, 8, give, 0)
        piece = pl.ds(theirs * 8, 8)
        rstart(d, xs.at[piece], xr.at[piece], sib)

    give_piece(1)
    give_piece(3)

    def chip_sum(si, fi, h):
        return own_sum(blk(c, si, fi) + h).astype(F32) + xr[lax.rem(fi, 4) * 8 + lax.rem(si, 4) * 2 + h].astype(F32)

    for d in order:
        fi = lax.rem(f + d, 4)
        rgot(d, xr.at[pl.ds(fi * 8, 8)])
        for e in (2, 1, 3):
            for h in range(2):
                r1s[d, e, h] = chip_sum(s + e, fi, h).astype(BF16)
            rstart(4 + 4 * d + e, r1s.at[d, e], r1r.at[d, e], speer[e])
        if d == 1:
            give_piece(2)
            tick(1, 1)
        if d == 3:
            give_piece(0)
    tick(0, 3)
    cgrad_ref[...] = jnp.zeros_like(cgrad_ref)

    def ctx_dot(n, _):
        cgrad_ref[...] += jnp.dot(chot_a[n], call_a[n], preferred_element_type=F32)
        return 0

    lax.fori_loop(0, 32, ctx_dot, 0)
    for cp in started:
        cp.wait_send()
    for ph in range(4):
        def drain(j, _):
            for cp in zcopies(ph, j):
                cp.wait_send()
            return 0

        lax.fori_loop(0, NB, drain, 0)
    legs = (1, 2, 3, 5, 6, 7, 8)
    for g in (0, 2):
        for k in legs:
            ccopies(g, k, False).wait_send()

    def plane_sum(d, h):
        total = chip_sum(s, f + d, h)
        for e in turns:
            total += r1r[d, e, h].astype(F32)
        return total

    for d in order:
        for e in turns:
            rgot(4 + 4 * d + e, r1r.at[d, e])
        for h in range(2):
            if d:
                r2s[d, h] = plane_sum(d, h).astype(BF16)
            else:
                igrad_ref[pl.ds(h * SIDE, SIDE), :] = plane_sum(d, h)
        if d:
            rstart(20 + d, r2s.at[d], r2r.at[d], fpeer[d])
        if d == 2:
            tick(1, 2)
    tick(1, 3)
    for n in range(8):
        rows = call_b[pl.ds(4 * n, 4)].reshape(SIDE, WIDTH)
        cgrad_ref[...] += jnp.dot(chot_b[n], rows, preferred_element_type=F32)
    for d in turns:
        rgot(20 + d, r2r.at[d])
        igrad_ref[...] += r2r[d].reshape(2 * SIDE, WIDTH).astype(F32)

    results[1].start()
    results[2].start()
    for cp in rcs:
        cp.wait_send()
    for k in legs:
        ccopies(1, k, False).wait_send()
    for cp in results:
        cp.wait()


def hand_over(*refs):
    srcs, dsts, bufs, sem = refs[:3], refs[3:6], refs[6:9], refs[9]
    reads = [pltpu.make_async_copy(a, b, sem.at[0, k]) for k, (a, b) in enumerate(zip(srcs, bufs))]
    writes = [pltpu.make_async_copy(a, b, sem.at[1, k]) for k, (a, b) in enumerate(zip(bufs, dsts))]
    for cp in reads:
        cp.start()
    for a, b in zip(reads, writes):
        a.wait()
        b.start()
    for cp in writes:
        cp.wait()


def local(
    user_factor,
    item_factor,
    context_factor,
    tile_user,
    tile_item,
    tile_context,
    tile_count,
    tile_mask,
    item_slot,
):
    n = tile_user.shape[0]
    nblocks = item_slot.shape[0]
    nctx = context_factor.shape[0]
    ids = jnp.arange(n, dtype=jnp.int32)
    hot_id = (tile_item[:, None] == jnp.arange(nblocks)[None, :]).astype(jnp.int32)
    slots = jnp.sum(hot_id * item_slot[None, :], axis=1)

    def place_of(block):
        owner, half = block // 2, block % 2
        core, xi, yi = owner % 2, owner // 8, (owner // 2) % 4
        fi = jnp.where(core == 0, xi, yi)
        si = jnp.where(core == 0, yi, xi)
        return ((core * 4 + si) * 4 + fi) * 2 + half

    place = place_of(slots)
    key = place * n + ids
    rank = jnp.sum((key[None, :] < key[:, None]).astype(jnp.int32), axis=1)
    pick = (rank[None, :] == ids[:, None]).astype(jnp.int32)
    live = (ids < tile_count[0]).astype(jnp.int32)
    vals = jnp.stack([place, tile_user, ids, live, tile_context])
    ordered = jnp.sum(pick[None] * vals[:, None, :], axis=2)
    place_s, ctx_s = ordered[PLACE], ordered[CTXT]
    before = jnp.concatenate([jnp.full((1,), -1, jnp.int32), place_s[:-1]])
    keep = (place_s == before).astype(jnp.int32)
    last = jnp.maximum(jnp.sum((place[None, :] <= ids[:, None]).astype(jnp.int32), axis=1) - 1, 0)
    has = jnp.any(place[None, :] == ids[:, None], axis=1).astype(jnp.int32)
    meta = jnp.concatenate([ordered, jnp.stack([keep, last, has])])
    rows = jnp.stack([ctx_s, jnp.tile(ctx_s[ROWS_A:], n // ROWS_B)])
    ids16 = jnp.pad(rows, ((0, 14), (0, 0))).astype(BF16)
    smem = pl.BlockSpec(memory_space=pltpu.SMEM)
    anywhere = pl.BlockSpec(memory_space=pl.ANY)
    tile2 = (SIDE, SIDE)
    wide = (SIDE, WIDTH)
    ugrad, igrad, cgrad = pl.pallas_call(
        kernel,
        out_shape=(
            jax.ShapeDtypeStruct((1024, WIDTH), F32),
            jax.ShapeDtypeStruct((2 * SIDE, WIDTH), F32),
            jax.ShapeDtypeStruct((nctx, WIDTH), F32),
        ),
        in_specs=[smem] + [anywhere] * 5,
        out_specs=(anywhere,) * 3,
        scratch_shapes=[
            pltpu.VMEM((8,) + wide, BF16),
            pltpu.VMEM((nctx, WIDTH), BF16),
            pltpu.VMEM((16, SIDE), BF16),
            pltpu.VMEM((1024, WIDTH), F32),
            pltpu.VMEM((2 * SIDE, WIDTH), F32),
            pltpu.VMEM((nctx, WIDTH), F32),
            pltpu.VMEM((64,) + wide, BF16),
            pltpu.VMEM((n,) + tile2, jnp.int32),
            pltpu.VMEM((nctx, WIDTH), F32),
            pltpu.VMEM((4, 4, PER) + tile2, F32),
            pltpu.VMEM((NB, PER) + tile2, BF16),
            pltpu.VMEM((NB, 2, 2) + tile2, BF16),
            pltpu.VMEM((NB, 2, PER) + tile2, BF16),
            pltpu.VMEM((NB, 2, PER) + tile2, BF16),
            pltpu.VMEM((NB, 4, PER) + tile2, BF16),
            pltpu.VMEM(wide, F32),
            pltpu.VMEM((n,) + wide, BF16),
            pltpu.VMEM((1024, PER * SIDE), BF16),
            pltpu.VMEM((PER * SIDE, WIDTH), BF16),
            pltpu.VMEM(wide, F32),
            pltpu.VMEM((32,) + wide, BF16),
            pltpu.VMEM((32, 32, WIDTH), BF16),
            pltpu.VMEM((32, 16, SIDE), BF16),
            pltpu.VMEM((32, nctx, SIDE), BF16),
            pltpu.VMEM((8, nctx, SIDE), BF16),
            pltpu.VMEM((32,) + wide, BF16),
            pltpu.VMEM((32,) + wide, BF16),
            pltpu.VMEM((4, 4, 2) + wide, BF16),
            pltpu.VMEM((4, 4, 2) + wide, BF16),
            pltpu.VMEM((4, 2) + wide, BF16),
            pltpu.VMEM((4, 2) + wide, BF16),
            pltpu.SemaphoreType.DMA((5,)),
            pltpu.SemaphoreType.DMA((3,)),
            pltpu.SemaphoreType.DMA((27,)),
            pltpu.SemaphoreType.DMA((27,)),
            pltpu.SemaphoreType.DMA((4, NB, 2)),
            pltpu.SemaphoreType.DMA((4, NB, 2)),
            pltpu.SemaphoreType.DMA((3, 9)),
            pltpu.SemaphoreType.DMA((3, 9)),
            pltpu.SemaphoreType.DMA((24,)),
            pltpu.SemaphoreType.DMA((24,)),
        ],
        compiler_params=pltpu.CompilerParams(
            collective_id=0, has_side_effects=True, vmem_limit_bytes=62 * 1024 * 1024
        ),
        cost_estimate=pl.CostEstimate(flops=10_000_000_000, bytes_accessed=20_000_000, transcendentals=0),
    )(
        meta,
        user_factor.reshape(-1, SIDE, WIDTH),
        item_factor.reshape(-1, SIDE, WIDTH),
        context_factor,
        ids16,
        tile_mask,
    )
    return pl.pallas_call(
        hand_over,
        out_shape=tuple(jax.ShapeDtypeStruct(a.shape, a.dtype) for a in (ugrad, igrad, cgrad)),
        in_specs=[anywhere] * 3,
        out_specs=(anywhere,) * 3,
        scratch_shapes=[pltpu.VMEM(a.shape, a.dtype) for a in (ugrad, igrad, cgrad)]
        + [pltpu.SemaphoreType.DMA((2, 3))],
    )(ugrad, igrad, cgrad)


def solution(mesh):
    return jax.shard_map(
        local,
        mesh=mesh,
        in_specs=(
            P("tiles", "rank"),
            P("tiles", "rank"),
            P(None, "rank"),
            P("tiles"),
            P("tiles"),
            P("tiles"),
            P("tiles"),
            P("tiles", None, None),
            P(),
        ),
        out_specs=(P("tiles", "rank"), P("tiles", "rank"), P(None, "rank")),
        check_vma=False,
    )
```

```python
import functools

import jax
import jax.numpy as jnp
from jax import lax
from jax.experimental import pallas as pl
from jax.experimental.pallas import tpu as pltpu
from jax.sharding import PartitionSpec as P

MESH = pl.DeviceIdType.MESH
BF16 = jnp.bfloat16
F32 = jnp.float32
NB = 8
PER = 4
SIDE = 128
WIDTH = 256
ROWS_B = 32
ROWS_A = SIDE - ROWS_B
PLACE, USER, PERM, LIVE, CTXT, KEEP, LAST, HAS = range(8)


def kernel(
    meta_ref,
    users_in,
    shard_in,
    context_in,
    ids_in,
    mask_in,
    ugrad_out,
    igrad_out,
    cgrad_out,
    users_ref,
    context_ref,
    ids_ref,
    ugrad_ref,
    igrad_ref,
    cgrad_ref,
    items,
    mask,
    ctx32,
    part,
    send1,
    recv1,
    send2,
    recv2,
    resid,
    run,
    segs,
    ahot,
    icb,
    cterm,
    call_a,
    call_b,
    idall,
    chot_a,
    chot_b,
    xs,
    xr,
    r1s,
    r1r,
    r2s,
    r2r,
    in_sem,
    out_sem,
    ag_send,
    ag_recv,
    z_send,
    z_recv,
    c_send,
    c_recv,
    r_send,
    r_recv,
):
    z = lax.axis_index("rank")
    t = lax.axis_index("tiles")
    c = lax.rem(t, 2)
    y = lax.rem(t // 2, 4)
    x = t // 8
    f = x * (1 - c) + y * c
    s = y * (1 - c) + x * c

    def dev(fi, si):
        fi, si = lax.rem(fi + 4, 4), lax.rem(si + 4, 4)
        xi = fi * (1 - c) + si * c
        yi = si * (1 - c) + fi * c
        return {"rank": z, "tiles": (xi * 4 + yi) * 2 + c}

    def devz(d):
        return {"rank": lax.rem(z + d + 4, 4), "tiles": t}

    sib = {"rank": z, "tiles": t + 1 - 2 * c}
    turns = (1, 3, 2)
    fpeer = {d: dev(f + d, s) for d in turns}
    speer = {d: dev(f, s + d) for d in turns}
    partners = tuple(fpeer.values()) + tuple(speer.values()) + (devz(1), devz(-1), sib)
    mine = ((c * 4 + s) * 4 + f) * 2
    fetch = [
        pltpu.make_async_copy(src, dst, in_sem.at[k])
        for k, (src, dst) in enumerate(
            (
                (shard_in, items.at[pl.ds(mine, 2)]),
                (context_in, context_ref),
                (ids_in, ids_ref),
                (users_in, users_ref),
                (mask_in, mask),
            )
        )
    ]
    for cp in fetch:
        cp.start()
    barrier = pltpu.get_barrier_semaphore()
    for p in partners:
        pl.semaphore_signal(barrier, inc=1, device_id=p, device_id_type=MESH)
    pl.semaphore_wait(barrier, len(partners))

    def rcopy(src, dst, ss, rs, to):
        return pltpu.make_async_remote_copy(
            src_ref=src, dst_ref=dst, send_sem=ss, recv_sem=rs, device_id=to, device_id_type=MESH
        )

    started = []

    def blk(ci, si, fi):
        return ((ci * 4 + lax.rem(si + 4, 4)) * 4 + lax.rem(fi + 4, 4)) * 2

    def ag(k, start, size, to):
        view = items.at[pl.ds(start, size)]
        cp = rcopy(view, view, ag_send.at[k], ag_recv.at[k], to)
        cp.start()
        started.append(cp)

    def got(k, start, size):
        view = items.at[pl.ds(start, size)]
        rcopy(view, view, ag_send.at[k], ag_recv.at[k], sib).wait_recv()

    fetch[0].wait()
    for d in turns:
        ag(d, mine, 2, fpeer[d])
    for d in (1, 3):
        ag(4 + d, mine, 2, speer[d])
    fetch[1].wait()
    ctx32[...] = context_ref[...].astype(F32)
    ugrad_ref[...] = jnp.zeros_like(ugrad_ref)
    run[...] = jnp.zeros_like(run)
    call_a[...] = jnp.zeros_like(call_a)

    def relay(e):
        for d in (1, 3):
            h = d // 2
            got(4 + 4 * e + d, blk(c, s - d, f + e), 2)
            ag((4 + 4 * e + 2, 27 + e)[h], blk(c, s - d, f + e) + h, 1, speer[d])

    for d in turns:
        e = 4 - d
        got(d, blk(c, s, f + e), 2)
        for dd in turns if e == 2 else (1, 3):
            ag(4 + 4 * e + dd, blk(c, s, f + e), 2, speer[dd])
        if e != 2:
            relay(0 if e == 3 else 3)
    ag(20, blk(c, s, 0 * f), 8, sib)
    last = tuple(zip((0, 3, 1, 2), (22, 24, 25, 26)))
    for d in turns:
        if d == 1:
            relay(1)
        for e, k in last:
            if e == 2:
                got(4 + 4 * e + d, blk(c, s - d, f + e), 2)
            elif d == 2:
                got(4 + 4 * e + 2, blk(c, s - 2, f + e), 1)
                got(27 + e, blk(c, s - 2, f + e) + 1, 1)
            if d == 2:
                ag(k, blk(c, s - d, f + e), 2, sib)
        if d != 2:
            ag(20 + d, blk(c, s - d, 0 * f), 8, sib)
    for d in (0, 1, 3):
        got(20 + d, blk(1 - c, f - d, 0 * f), 8)
    for e, k in last:
        got(k, blk(1 - c, f - 2, s + e), 2)
    for cp in fetch[2:]:
        cp.wait()

    right, left = devz(1), devz(-1)

    def zcopies(ph, j):
        o = z
        if ph == 0:
            return (
                rcopy(send1.at[j, pl.ds(0, 2)], recv1.at[j, 0], z_send.at[ph, j, 0], z_recv.at[ph, j, 0], right),
                rcopy(send1.at[j, pl.ds(2, 2)], recv1.at[j, 1], z_send.at[ph, j, 1], z_recv.at[ph, j, 1], left),
            )
        if ph == 1:
            return (
                rcopy(send2.at[j, 0], recv2.at[j, 0], z_send.at[ph, j, 0], z_recv.at[ph, j, 0], right),
                rcopy(send2.at[j, 1], recv2.at[j, 1], z_send.at[ph, j, 1], z_recv.at[ph, j, 1], left),
            )
        if ph == 2:
            return (
                rcopy(resid.at[j, o], resid.at[j, o], z_send.at[ph, j, 0], z_recv.at[ph, j, 0], right),
                rcopy(resid.at[j, o], resid.at[j, o], z_send.at[ph, j, 1], z_recv.at[ph, j, 1], left),
            )
        lo, hi = lax.rem(z + 3, 4), lax.rem(z + 1, 4)
        a = resid.at[j, lo, pl.ds(0, 2)]
        b = resid.at[j, hi, pl.ds(2, 2)]
        return (
            rcopy(a, a, z_send.at[ph, j, 0], z_recv.at[ph, j, 0], right),
            rcopy(b, b, z_send.at[ph, j, 1], z_recv.at[ph, j, 1], left),
        )

    def zwait(ph, j):
        lo, hi, far = lax.rem(z + 3, 4), lax.rem(z + 1, 4), lax.rem(z + 2, 4)
        if ph == 0:
            views = (recv1.at[j, 0], recv1.at[j, 1])
        elif ph == 1:
            views = (recv2.at[j, 0], recv2.at[j, 1])
        elif ph == 2:
            views = (resid.at[j, lo], resid.at[j, hi])
        else:
            views = (resid.at[j, far, pl.ds(0, 2)], resid.at[j, far, pl.ds(2, 2)])
        for d in range(2):
            rcopy(views[d], views[d], z_send.at[ph, j, d], z_recv.at[ph, j, d], right).wait_recv()

    def item_context(p):
        it = items[meta_ref[PLACE, p]].astype(F32)
        return (it * ctx32[pl.ds(meta_ref[CTXT, p], 1), :]).astype(BF16)

    def predict(j):
        slot = lax.rem(j, 4)

        far = lax.rem(z + 2, 4)

        def tile(n, _):
            o, k = lax.rem(far + n // PER, 4), lax.rem(n, PER)
            p = j * 16 + o * PER + k
            pr = lax.dot_general(
                users_ref[meta_ref[USER, p]], item_context(p), (((1,), (1,)), ((), ())), preferred_element_type=F32
            )
            part[slot, o, k] = pr
            return 0

        lax.fori_loop(0, PER, tile, 0)
        send1[j] = part[slot, far].astype(BF16)
        for cp in zcopies(0, j):
            cp.start()
        lax.fori_loop(PER, 16, tile, 0)

    def combine(j):
        slot = lax.rem(j, 4)
        hi, lo = lax.rem(z + 1, 4), lax.rem(z + 3, 4)
        zwait(0, j)
        send2[j, 0, pl.ds(0, 2)] = (part[slot, hi, pl.ds(0, 2)] + recv1[j, 0].astype(F32)).astype(BF16)
        send2[j, 0, pl.ds(2, 2)] = part[slot, hi, pl.ds(2, 2)].astype(BF16)
        send2[j, 1, pl.ds(0, 2)] = part[slot, lo, pl.ds(0, 2)].astype(BF16)
        send2[j, 1, pl.ds(2, 2)] = (part[slot, lo, pl.ds(2, 2)] + recv1[j, 1].astype(F32)).astype(BF16)
        for cp in zcopies(1, j):
            cp.start()

    def weigh(j):
        slot = lax.rem(j, 4)
        zwait(1, j)
        for k in range(PER):
            p = j * 16 + z * PER + k
            pr = part[slot, z, k] + recv2[j, 0, k].astype(F32) + recv2[j, 1, k].astype(F32)
            m = mask[meta_ref[PERM, p]].astype(F32)
            resid[j, z, k] = (meta_ref[LIVE, p].astype(F32) * (1.0 + 4.0 * m) * (pr - m) * (1.0 / 128.0)).astype(BF16)
        for cp in zcopies(2, j):
            cp.start()

    def forward(j):
        zwait(2, j)
        for cp in zcopies(3, j):
            cp.start()

    def user_part(j, o):
        for k in range(PER):
            p = j * 16 + o * PER + k
            r = resid[j, o, k]
            u = meta_ref[USER, p]
            for b in range(8):
                ahot[pl.ds(b * SIDE, SIDE), pl.ds(k * SIDE, SIDE)] = jnp.where(u == b, r, jnp.zeros_like(r))
            icb[pl.ds(k * SIDE, SIDE), :] = item_context(p)
        ugrad_ref[...] += jnp.dot(ahot[...], icb[...], preferred_element_type=F32)

    def item_part(j, o):
        for k in range(PER):
            p = j * 16 + o * PER + k
            it = items[meta_ref[PLACE, p]].astype(F32)
            cr = ctx32[pl.ds(meta_ref[CTXT, p], 1), :]
            q = lax.dot_general(
                resid[j, o, k], users_ref[meta_ref[USER, p]], (((0,), (0,)), ((), ())), preferred_element_type=F32
            )
            cterm[pl.ds(p, 1), :] = jnp.sum(it * q, axis=0, keepdims=True)
            total = run[...] * meta_ref[KEEP, p].astype(F32) + q * cr
            run[...] = total
            segs[p] = total.astype(BF16)

    def gradients(j):
        def near(n, _):
            user_part(j, lax.rem(z + 3 + n, 4))
            return 0

        def group(o, _):
            item_part(j, o)
            return 0

        lax.fori_loop(0, 3, near, 0)
        zwait(3, j)
        lax.fori_loop(0, 4, group, 0)
        user_part(j, lax.rem(z + 2, 4))

    def ccopies(g, k, arriving):
        pos = lambda si, fi: (c * 4 + lax.rem(si + 4, 4)) * 4 + lax.rem(fi + 4, 4)
        if k < 4:
            at, count, to = (pos(s, f - k) if arriving else pos(s, f)), 1, fpeer[k]
        elif k < 8:
            at, count, to = (pos(s - (k - 4), 0 * f) if arriving else pos(s, 0 * f)), 4, speer[k - 4]
        else:
            at, count, to = ((1 - c) * 16 if arriving else c * 16), 16, sib
        if g == 0:
            a = call_a.at[pl.ds(at, count), pl.ds(0, ROWS_A)]
        else:
            a = (call_b if g == 1 else idall).at[pl.ds(at, count)]
        return rcopy(a, a, c_send.at[g, k], c_recv.at[g, k], to)

    def tick(g, n):
        own = (c * 4 + s) * 4 + f
        if n == 0:
            if g == 0:
                call_a[own, pl.ds(0, ROWS_A)] = cterm[pl.ds(0, ROWS_A), :].astype(BF16)
            elif g == 1:
                call_b[own] = cterm[pl.ds(ROWS_A, ROWS_B), :].astype(BF16)
            else:
                row = lax.broadcasted_iota(jnp.int32, (16, SIDE), 0)
                lane = lax.broadcasted_iota(jnp.int32, (16, SIDE), 1)
                hidden = (row == 1) & (lane // ROWS_B != f)
                idall[own] = jnp.where(hidden, 0.0, ids_ref[...].astype(F32)).astype(BF16)
        else:
            for d in turns if n < 3 else (0,):
                ccopies(g, 4 * (n - 1) + d, True).wait_recv()
        if n < 3:
            for d in turns if n < 2 else (0,):
                ccopies(g, 4 * n + d, False).start()

    def hot(ids):
        rows = lax.broadcasted_iota(jnp.int32, (WIDTH, SIDE), 0).astype(F32)
        return jnp.where(rows == ids, 1.0, 0.0).astype(BF16)

    def hots(n, _):
        rest = jnp.zeros((1, SIDE), F32)
        for k in range(4):
            both = idall[n * 4 + k].astype(F32)
            chot_a[n * 4 + k] = hot(both[0:1, :])
            rest += both[1:2, :]
        chot_b[n] = hot(rest)
        return 0

    def step(i, _):
        for n in range(4):

            @pl.when(i == 2 + n)
            def _():
                tick(2, n)

        @pl.when(i == NB + 3)
        def _():
            tick(0, 2)

        @pl.when(i < NB)
        def _():
            predict(i)

        @pl.when((i >= 1) & (i < NB + 1))
        def _():
            combine(i - 1)

        @pl.when((i >= 2) & (i < NB + 2))
        def _():
            weigh(i - 2)

        @pl.when((i >= 3) & (i < NB + 3))
        def _():
            forward(i - 3)

        @pl.when(i >= 4)
        def _():
            gradients(i - 4)

        @pl.when(i == NB + 1)
        def _():
            lax.fori_loop(0, 8, hots, 0)
            tick(0, 0)

        @pl.when(i == NB + 2)
        def _():
            tick(0, 1)

        return 0

    lax.fori_loop(0, NB + 4, step, 0)

    def rc(k, src, dst, to):
        return rcopy(src, dst, r_send.at[k], r_recv.at[k], to)

    def rgot(k, dst):
        rc(k, dst, dst, sib).wait_recv()

    def own_sum(b):
        v = segs[meta_ref[LAST, b]]
        return jnp.where(meta_ref[HAS, b] > 0, v, jnp.zeros_like(v))

    rcs = []

    def rstart(k, src, dst, to):
        cp = rc(k, src, dst, to)
        cp.start()
        rcs.append(cp)

    tick(1, 0)
    results = [
        pltpu.make_async_copy(src, dst, out_sem.at[k])
        for k, (src, dst) in enumerate(((ugrad_ref, ugrad_out), (igrad_ref, igrad_out), (cgrad_ref, cgrad_out)))
    ]
    results[0].start()
    order = (1, 3, 2, 0)

    def give_piece(d):
        theirs = lax.rem(s + d, 4)

        def give(n, _):
            xs[theirs * 8 + n] = own_sum(blk(1 - c, n // 2, theirs) + lax.rem(n, 2))
            return 0

        lax.fori_loop(0, 8, give, 0)
        piece = pl.ds(theirs * 8, 8)
        rstart(d, xs.at[piece], xr.at[piece], sib)

    give_piece(1)
    give_piece(3)

    def chip_sum(si, fi, h):
        return own_sum(blk(c, si, fi) + h).astype(F32) + xr[lax.rem(fi, 4) * 8 + lax.rem(si, 4) * 2 + h].astype(F32)

    for d in order:
        fi = lax.rem(f + d, 4)
        rgot(d, xr.at[pl.ds(fi * 8, 8)])
        for e in (2, 1, 3):
            for h in range(2):
                r1s[d, e, h] = chip_sum(s + e, fi, h).astype(BF16)
            rstart(4 + 4 * d + e, r1s.at[d, e], r1r.at[d, e], speer[e])
        if d == 1:
            give_piece(2)
            tick(1, 1)
        if d == 3:
            give_piece(0)
    tick(0, 3)
    cgrad_ref[...] = jnp.zeros_like(cgrad_ref)

    def ctx_dot(n, _):
        cgrad_ref[...] += jnp.dot(chot_a[n], call_a[n], preferred_element_type=F32)
        return 0

    lax.fori_loop(0, 32, ctx_dot, 0)
    for cp in started:
        cp.wait_send()
    for ph in range(4):
        def drain(j, _):
            for cp in zcopies(ph, j):
                cp.wait_send()
            return 0

        lax.fori_loop(0, NB, drain, 0)
    legs = (1, 2, 3, 5, 6, 7, 8)
    for g in (0, 2):
        for k in legs:
            ccopies(g, k, False).wait_send()

    def plane_sum(d, h):
        total = chip_sum(s, f + d, h)
        for e in turns:
            total += r1r[d, e, h].astype(F32)
        return total

    for d in order:
        for e in turns:
            rgot(4 + 4 * d + e, r1r.at[d, e])
        for h in range(2):
            if d:
                r2s[d, h] = plane_sum(d, h).astype(BF16)
            else:
                igrad_ref[pl.ds(h * SIDE, SIDE), :] = plane_sum(d, h)
        if d:
            rstart(20 + d, r2s.at[d], r2r.at[d], fpeer[d])
        if d == 2:
            tick(1, 2)
    tick(1, 3)
    for n in range(8):
        rows = call_b[pl.ds(4 * n, 4)].reshape(SIDE, WIDTH)
        cgrad_ref[...] += jnp.dot(chot_b[n], rows, preferred_element_type=F32)
    for d in turns:
        rgot(20 + d, r2r.at[d])
        igrad_ref[...] += r2r[d].reshape(2 * SIDE, WIDTH).astype(F32)

    results[1].start()
    results[2].start()
    for cp in rcs:
        cp.wait_send()
    for k in legs:
        ccopies(1, k, False).wait_send()
    for cp in results:
        cp.wait()


def hand_over(*refs):
    srcs, dsts, bufs, sem = refs[:3], refs[3:6], refs[6:9], refs[9]
    reads = [pltpu.make_async_copy(a, b, sem.at[0, k]) for k, (a, b) in enumerate(zip(srcs, bufs))]
    writes = [pltpu.make_async_copy(a, b, sem.at[1, k]) for k, (a, b) in enumerate(zip(bufs, dsts))]
    for cp in reads:
        cp.start()
    for a, b in zip(reads, writes):
        a.wait()
        b.start()
    for cp in writes:
        cp.wait()


def local(
    user_factor,
    item_factor,
    context_factor,
    tile_user,
    tile_item,
    tile_context,
    tile_count,
    tile_mask,
    item_slot,
):
    n = tile_user.shape[0]
    nblocks = item_slot.shape[0]
    nctx = context_factor.shape[0]
    ids = jnp.arange(n, dtype=jnp.int32)
    hot_id = (tile_item[:, None] == jnp.arange(nblocks)[None, :]).astype(jnp.int32)
    slots = jnp.sum(hot_id * item_slot[None, :], axis=1)

    def place_of(block):
        owner, half = block // 2, block % 2
        core, xi, yi = owner % 2, owner // 8, (owner // 2) % 4
        fi = jnp.where(core == 0, xi, yi)
        si = jnp.where(core == 0, yi, xi)
        return ((core * 4 + si) * 4 + fi) * 2 + half

    place = place_of(slots)
    key = place * n + ids
    rank = jnp.sum((key[None, :] < key[:, None]).astype(jnp.int32), axis=1)
    pick = (rank[None, :] == ids[:, None]).astype(jnp.int32)
    live = (ids < tile_count[0]).astype(jnp.int32)
    vals = jnp.stack([place, tile_user, ids, live, tile_context])
    ordered = jnp.sum(pick[None] * vals[:, None, :], axis=2)
    place_s, ctx_s = ordered[PLACE], ordered[CTXT]
    before = jnp.concatenate([jnp.full((1,), -1, jnp.int32), place_s[:-1]])
    keep = (place_s == before).astype(jnp.int32)
    last = jnp.maximum(jnp.sum((place[None, :] <= ids[:, None]).astype(jnp.int32), axis=1) - 1, 0)
    has = jnp.any(place[None, :] == ids[:, None], axis=1).astype(jnp.int32)
    meta = jnp.concatenate([ordered, jnp.stack([keep, last, has])])
    rows = jnp.stack([ctx_s, jnp.tile(ctx_s[ROWS_A:], n // ROWS_B)])
    ids16 = jnp.pad(rows, ((0, 14), (0, 0))).astype(BF16)
    smem = pl.BlockSpec(memory_space=pltpu.SMEM)
    anywhere = pl.BlockSpec(memory_space=pl.ANY)
    tile2 = (SIDE, SIDE)
    wide = (SIDE, WIDTH)
    ugrad, igrad, cgrad = pl.pallas_call(
        kernel,
        out_shape=(
            jax.ShapeDtypeStruct((1024, WIDTH), F32),
            jax.ShapeDtypeStruct((2 * SIDE, WIDTH), F32),
            jax.ShapeDtypeStruct((nctx, WIDTH), F32),
        ),
        in_specs=[smem] + [anywhere] * 5,
        out_specs=(anywhere,) * 3,
        scratch_shapes=[
            pltpu.VMEM((8,) + wide, BF16),
            pltpu.VMEM((nctx, WIDTH), BF16),
            pltpu.VMEM((16, SIDE), BF16),
            pltpu.VMEM((1024, WIDTH), F32),
            pltpu.VMEM((2 * SIDE, WIDTH), F32),
            pltpu.VMEM((nctx, WIDTH), F32),
            pltpu.VMEM((64,) + wide, BF16),
            pltpu.VMEM((n,) + tile2, jnp.int32),
            pltpu.VMEM((nctx, WIDTH), F32),
            pltpu.VMEM((4, 4, PER) + tile2, F32),
            pltpu.VMEM((NB, PER) + tile2, BF16),
            pltpu.VMEM((NB, 2, 2) + tile2, BF16),
            pltpu.VMEM((NB, 2, PER) + tile2, BF16),
            pltpu.VMEM((NB, 2, PER) + tile2, BF16),
            pltpu.VMEM((NB, 4, PER) + tile2, BF16),
            pltpu.VMEM(wide, F32),
            pltpu.VMEM((n,) + wide, BF16),
            pltpu.VMEM((1024, PER * SIDE), BF16),
            pltpu.VMEM((PER * SIDE, WIDTH), BF16),
            pltpu.VMEM(wide, F32),
            pltpu.VMEM((32,) + wide, BF16),
            pltpu.VMEM((32, 32, WIDTH), BF16),
            pltpu.VMEM((32, 16, SIDE), BF16),
            pltpu.VMEM((32, nctx, SIDE), BF16),
            pltpu.VMEM((8, nctx, SIDE), BF16),
            pltpu.VMEM((32,) + wide, BF16),
            pltpu.VMEM((32,) + wide, BF16),
            pltpu.VMEM((4, 4, 2) + wide, BF16),
            pltpu.VMEM((4, 4, 2) + wide, BF16),
            pltpu.VMEM((4, 2) + wide, BF16),
            pltpu.VMEM((4, 2) + wide, BF16),
            pltpu.SemaphoreType.DMA((5,)),
            pltpu.SemaphoreType.DMA((3,)),
            pltpu.SemaphoreType.DMA((31,)),
            pltpu.SemaphoreType.DMA((31,)),
            pltpu.SemaphoreType.DMA((4, NB, 2)),
            pltpu.SemaphoreType.DMA((4, NB, 2)),
            pltpu.SemaphoreType.DMA((3, 9)),
            pltpu.SemaphoreType.DMA((3, 9)),
            pltpu.SemaphoreType.DMA((24,)),
            pltpu.SemaphoreType.DMA((24,)),
        ],
        compiler_params=pltpu.CompilerParams(
            collective_id=0, has_side_effects=True, vmem_limit_bytes=62 * 1024 * 1024
        ),
        cost_estimate=pl.CostEstimate(flops=10_000_000_000, bytes_accessed=20_000_000, transcendentals=0),
    )(
        meta,
        user_factor.reshape(-1, SIDE, WIDTH),
        item_factor.reshape(-1, SIDE, WIDTH),
        context_factor,
        ids16,
        tile_mask,
    )
    return pl.pallas_call(
        hand_over,
        out_shape=tuple(jax.ShapeDtypeStruct(a.shape, a.dtype) for a in (ugrad, igrad, cgrad)),
        in_specs=[anywhere] * 3,
        out_specs=(anywhere,) * 3,
        scratch_shapes=[pltpu.VMEM(a.shape, a.dtype) for a in (ugrad, igrad, cgrad)]
        + [pltpu.SemaphoreType.DMA((2, 3))],
    )(ugrad, igrad, cgrad)


def solution(mesh):
    return jax.shard_map(
        local,
        mesh=mesh,
        in_specs=(
            P("tiles", "rank"),
            P("tiles", "rank"),
            P(None, "rank"),
            P("tiles"),
            P("tiles"),
            P("tiles"),
            P("tiles"),
            P("tiles", None, None),
            P(),
        ),
        out_specs=(P("tiles", "rank"), P("tiles", "rank"), P(None, "rank")),
        check_vma=False,
    )
```
